128 devices in a mesh: row: 8 (over x_lo, y), col: 16 (over x_hi, z, core).
Axes of the slice: x: 4 (x_hi: 2, x_lo: 2; x = x_hi * 2 + x_lo), y: 4, z: 4, core: 2. Of those that a mesh axis runs over, the one named last changes fastest.
Arguments:
- pair: bfloat16 [512, 512, 128], P('row', 'col'), may hold values from -6 to 6
- grad_out: bfloat16 [512, 512, 128], P('row', 'col'), may hold values from -6 to 6
- norm_gain: float32 [128], replicated, may hold values from 0.25 to 1.75
- norm_shift: float32 [128], replicated, may hold values from -3 to 3
- w_query: bfloat16 [128, 128], replicated
- w_key: bfloat16 [128, 128], replicated, may hold values from -0.5 to 0.5
- w_value: bfloat16 [128, 128], replicated, may hold values from -0.5 to 0.5
- w_gate: bfloat16 [128, 128], replicated, may hold values from -0.5 to 0.5
- w_bias: bfloat16 [128, 4], replicated, may hold values from -1 to 1
- w_out: bfloat16 [128, 128], replicated, may hold values from -0.5 to 0.5
Outputs:
- d_pair: bfloat16 [512, 512, 128], P('row', 'col')
- d_gain: float32 [128], replicated
- d_shift: float32 [128], replicated
- d_query: float32 [128, 128], replicated
- d_key: float32 [128, 128], replicated
- d_value: float32 [128, 128], replicated
- d_gate: float32 [128, 128], replicated
- d_bias: float32 [128, 4], replicated
- d_out: float32 [128, 128], replicated
The draws below stay inside these ranges and needn't reach their ends.
All inputs are finite; a program needn't handle non-finite values.
Results may differ from the reference program's by a relative error of at most 0.012.
The reference program's roundings to bfloat16 on the way count: a program that leaves them out, or rounds other values in their place, can miss the bound.
Values may be sent and summed in bfloat16 or wider, within the bound.
No kernel may reach another device: no remote copies, remote signals or barrier semaphores. Data moves between devices by JAX's collectives and lax.ppermute only.
A program may use at most 192 MiB of HBM per device.

```python
import jax
import jax.numpy as jnp
from jax import lax

C = 128
H = 4
DH = 32
N = 512


def draw_w_query(key, part):
    key = jax.random.fold_in(key, 11)
    base_key = jax.random.fold_in(key, 0)
    base = jax.random.normal(base_key, (C, C), jnp.float32) * C ** (-0.5)
    return base.astype(jnp.bfloat16)


def shard_levels(stream_key, shape, shards, smallest, high):
    def one(position, parts):
        draws = jax.random.uniform(jax.random.fold_in(jax.random.fold_in(stream_key, 6), position), (parts,), jnp.float32, smallest / len(shards), high / len(shards))
        return jnp.repeat(jnp.exp(draws), shape[position] // parts).reshape((-1,) + (1,) * (len(shape) - position - 1))

    gain = one(*shards[0])
    for cut in shards[1:]:
        gain = gain * one(*cut)
    return gain


def scatter_about(stream_key, dims, width, bound, cuts=(), held_as=jnp.bfloat16):
    level = shard_levels(stream_key, dims, cuts, -0.22, 0.18) if cuts else 1.0
    result = jax.random.normal(stream_key, dims, jnp.float32) * width * level
    return jnp.minimum(jnp.maximum(result, -bound), bound).astype(held_as)


def setup_inputs(seed: int = 0) -> dict:
    seeds = jax.random.split(jax.random.key(seed), 11)
    pair = scatter_about(seeds[0], (N, N, C), 1.0, 6.0, ((0, 8), (1, 16)))
    grad_out = scatter_about(seeds[1], (N, N, C), 1.0, 6.0, ((0, 8), (1, 16)))
    norm_gain = jnp.clip(1.0 + 0.15 * jax.random.normal(seeds[2], (C,), jnp.float32), 0.25, 1.75)
    norm_shift = scatter_about(seeds[3], (C,), 0.5, 3.0, (), jnp.float32)
    w_query = draw_w_query(jax.random.fold_in(seeds[10], 71), 0)
    w_key = scatter_about(seeds[5], (C, C), C ** -0.5, 0.5)
    w_value = scatter_about(seeds[6], (C, C), C ** -0.5, 0.5)
    w_gate = scatter_about(seeds[7], (C, C), C ** -0.5, 0.5)
    w_bias = scatter_about(seeds[8], (C, H), 0.18, 1.0)
    w_out = scatter_about(seeds[9], (C, C), C ** -0.5, 0.5)
    return dict(pair=pair, grad_out=grad_out, norm_gain=norm_gain, norm_shift=norm_shift, w_query=w_query, w_key=w_key, w_value=w_value, w_gate=w_gate, w_bias=w_bias, w_out=w_out)


EPS = 1e-05

def layer_norm(pair, norm_gain, norm_shift):
    values = pair.astype(jnp.float32)
    center = values - lax.optimization_barrier(jnp.mean(values, axis=-1, keepdims=True))
    rstd = lax.rsqrt(lax.optimization_barrier(jnp.mean(center * center, axis=-1, keepdims=True)) + EPS)
    normed = center * rstd
    return ((normed * norm_gain + norm_shift).astype(jnp.bfloat16), normed, rstd)

def project(values, weight):
    return jnp.einsum('...e,ce->...c', values, weight.astype(jnp.float32), precision=lax.Precision.HIGHEST)

def outer_sum(inputs, grads):
    return jnp.einsum('ijc,ijd->cd', inputs.astype(jnp.float32), grads, precision=lax.Precision.HIGHEST)

def mixed(form, left, right):
    return jnp.einsum(form, left.astype(jnp.float32), right.astype(jnp.float32), precision=lax.Precision.HIGHEST)

def attend_grad(x_query, x_keys, bias, grad_rows, w_query, w_key, w_value, w_gate, w_out):
    rows, cols = (x_query.shape[0], x_query.shape[1])
    keys = x_keys.shape[1]
    scale = DH ** (-0.5)
    query = mixed('ijc,cd->ijd', x_query, w_query).astype(jnp.bfloat16).reshape(rows, cols, H, DH)
    key_h = mixed('ijc,cd->ijd', x_keys, w_key).astype(jnp.bfloat16).reshape(rows, keys, H, DH)
    value_h = mixed('ijc,cd->ijd', x_keys, w_value).astype(jnp.bfloat16).reshape(rows, keys, H, DH)
    gate = jax.nn.sigmoid(mixed('ijc,cd->ijd', x_query, w_gate))
    scores = mixed('ijhd,ikhd->ihjk', query, key_h) * scale + bias[None].astype(jnp.float32)
    expo = jnp.exp(scores - lax.optimization_barrier(jnp.max(scores, axis=-1, keepdims=True)))
    probs = expo / lax.optimization_barrier(jnp.sum(expo, axis=-1, keepdims=True))
    probs_b = probs.astype(jnp.bfloat16)
    attended = mixed('ihjk,ikhd->ijhd', probs_b, value_h)
    flat = attended.reshape(rows, cols, H * DH)
    gated = (gate * flat).astype(jnp.bfloat16)
    dgated = mixed('ijd,cd->ijc', grad_rows, w_out)
    d_out = mixed('ijc,ijd->cd', gated, grad_rows)
    dob = (dgated * gate).astype(jnp.bfloat16)
    dgraw = dgated * flat * gate * (1.0 - gate)
    dob_h = dob.reshape(rows, cols, H, DH)
    dprob = mixed('ijhd,ikhd->ihjk', dob_h, value_h)
    dvalue = mixed('ihjk,ijhd->ikhd', probs_b, dob_h)
    delta = lax.optimization_barrier(jnp.sum(dob_h.astype(jnp.float32) * attended, axis=-1)).transpose(0, 2, 1)[..., None]
    dscore = probs * (dprob - delta)
    dscore_b = dscore.astype(jnp.bfloat16)
    dquery = mixed('ihjk,ikhd->ijhd', dscore_b, key_h) * scale
    dkey = mixed('ihjk,ijhd->ikhd', dscore_b, query) * scale
    dbias = lax.optimization_barrier(jnp.sum(dscore, axis=0))
    dquery = dquery.reshape(rows, cols, H * DH)
    dx_query = project(dquery, w_query) + project(dgraw, w_gate)
    return (dx_query, dkey.reshape(rows, keys, H * DH), dvalue.reshape(rows, keys, H * DH), dbias, outer_sum(x_query, dquery), outer_sum(x_query, dgraw), d_out)

def reference(pair, grad_out, norm_gain, norm_shift, w_query, w_key, w_value, w_gate, w_bias, w_out):
    x, normed, rstd = layer_norm(pair, norm_gain, norm_shift)
    bias = mixed('ijc,ch->hij', x, w_bias).astype(jnp.bfloat16)
    block_rows = min(16, N)
    count = N // block_rows

    def one_block(carry, index):
        start = (index * block_rows).astype(jnp.int32)
        x_block = lax.dynamic_slice_in_dim(x, start, block_rows, 0)
        g_block = lax.dynamic_slice_in_dim(grad_out, start, block_rows, 0)
        dx_q, dkey, dvalue, dbias, dwq, dwg, dwo = attend_grad(x_block, x_block, bias, g_block, w_query, w_key, w_value, w_gate, w_out)
        dx_block = dx_q + project(dkey, w_key) + project(dvalue, w_value)
        dwk = outer_sum(x_block, dkey)
        dwv = outer_sum(x_block, dvalue)
        sums = (carry[0] + dbias, carry[1] + dwq, carry[2] + dwk, carry[3] + dwv, carry[4] + dwg, carry[5] + dwo)
        return (sums, dx_block)
    square = jnp.zeros((C, C), jnp.float32)
    init = (jnp.zeros((H, N, N), jnp.float32), square, square, square, square, square)
    sums, dx_blocks = lax.scan(one_block, init, jnp.arange(count, dtype=jnp.int32))
    dbias, d_query, d_key, d_value, d_gate, d_out = sums
    dx = dx_blocks.reshape(N, N, C)
    dbias_pairs = dbias.transpose(1, 2, 0)
    dx = dx + project(dbias_pairs, w_bias)
    d_bias = outer_sum(x, dbias_pairs)
    d_gain = lax.optimization_barrier(jnp.sum(dx * normed, axis=(0, 1)))
    d_shift = lax.optimization_barrier(jnp.sum(dx, axis=(0, 1)))
    dnorm = dx * norm_gain
    d_pair = rstd * (dnorm - lax.optimization_barrier(jnp.mean(dnorm, axis=-1, keepdims=True)) - normed * lax.optimization_barrier(jnp.mean(dnorm * normed, axis=-1, keepdims=True)))
    return (d_pair.astype(jnp.bfloat16), d_gain, d_shift, d_query, d_key, d_value, d_gate, d_bias, d_out)
```

```python
import jax
import jax.numpy as jnp
from jax import lax
from jax.experimental import pallas as pl
from jax.experimental.pallas import tpu as pltpu
from jax.sharding import PartitionSpec as P

H = 4
DH = 32
C = 128
EPS = 1e-05
LOG2E = 1.4426950408889634
F32 = jnp.float32
BF16 = jnp.bfloat16
VMEM_LIMIT = 56 * 1024 * 1024


def dot_nn(a, b):
    return lax.dot_general(a, b, (((1,), (0,)), ((), ())), preferred_element_type=F32)


def dot_nt(a, b):
    return lax.dot_general(a, b, (((1,), (1,)), ((), ())), preferred_element_type=F32)


def dot_tn(a, b):
    return lax.dot_general(a, b, (((0,), (0,)), ((), ())), preferred_element_type=F32)


def normalize(values):
    center = values - jnp.mean(values, axis=-1, keepdims=True)
    rstd = lax.rsqrt(jnp.mean(center * center, axis=-1, keepdims=True) + EPS)
    return center * rstd, rstd


def call(kernel, out_shape, n_in, scratch=(), smem=0):
    specs = [pl.BlockSpec(memory_space=pltpu.SMEM)] * smem
    specs += [pl.BlockSpec(memory_space=pltpu.VMEM)] * n_in
    outs = jax.tree.map(lambda _: pl.BlockSpec(memory_space=pltpu.VMEM), out_shape)
    return pl.pallas_call(
        kernel,
        out_shape=out_shape,
        in_specs=specs,
        out_specs=outs,
        scratch_shapes=list(scratch),
        compiler_params=pltpu.CompilerParams(vmem_limit_bytes=VMEM_LIMIT),
    )


def pack_kernel(pair_ref, grad_ref, gain_ref, shift_ref, wb_ref, out_ref, xt_ref, x_scr, b_scr):
    rows, cols = pair_ref.shape[0], pair_ref.shape[1]
    out_ref[:, 0, 0:cols, :] = pair_ref[...]
    out_ref[:, 1, 0:cols, :] = grad_ref[...]
    normed, _ = normalize(pair_ref[...].reshape(rows * cols, C).astype(F32))
    x_scr[...] = normed * gain_ref[...] + shift_ref[...]
    for k in range(cols):
        xt_ref[k * rows : (k + 1) * rows, :] = x_scr[pl.ds(k, rows, stride=cols), :].astype(BF16)
    bias = dot_nt(wb_ref[...], xt_ref[...])
    for pair in range(2):
        for k in range(cols):
            part = bias[2 * pair : 2 * pair + 2, k * rows : (k + 1) * rows]
            b_scr[k : k + 1, :] = jnp.concatenate([part[0:1], part[1:2]], axis=1)
        packed = b_scr[...].astype(BF16)
        out_ref[:, pair, cols : 2 * cols, :] = jnp.broadcast_to(packed[None], (rows, cols, C))


def attend_kernel(
    core_ref, mine_ref, other_ref, gain_ref, shift_ref, wq_ref, wk_ref, wv_ref, wg_ref, wo_ref,
    out_ref, bias_scr, acc_scr, w_scr, wacc_scr, d_scr,
):
    core = core_ref[0]
    groups, blocks, cols = 8, 16, 32
    n = blocks * cols
    scale = DH ** (-0.5)
    lane = lax.broadcasted_iota(jnp.int32, (n, C), 1)
    low = lane < 64

    for slot, ref in enumerate((wq_ref, wg_ref, wk_ref, wv_ref)):
        turned = jnp.transpose(ref[...].astype(F32)).astype(BF16)
        w_scr[slot * 64 : (slot + 1) * 64, :] = jnp.where(core == 0, turned[0:64], turned[64:128])
    w_scr[256:320, :] = jnp.where(core == 0, wo_ref[0:64, :], wo_ref[64:128, :])

    for r in range(0, groups, 2):
        b0 = mine_ref[r * blocks : (r + 1) * blocks, cols : 2 * cols, :].reshape(n, C).astype(F32)
        b1 = mine_ref[(r + 1) * blocks : (r + 2) * blocks, cols : 2 * cols, :].reshape(n, C)
        b1 = b1.astype(F32)
        sl = slice(r * 64, r * 64 + 128)
        bias_scr[0, :, sl] = jnp.where(low, b0, pltpu.roll(b1, 64, 1)) * LOG2E
        bias_scr[1, :, sl] = jnp.where(low, pltpu.roll(b0, 64, 1), b1) * LOG2E
    acc_scr[...] = jnp.zeros_like(acc_scr)
    wacc_scr[...] = jnp.zeros_like(wacc_scr)

    def one_row(r, carry):
        src = pl.ds(r * blocks, blocks)
        mine = mine_ref[src, 0:cols, :].reshape(n, C)
        other = other_ref[src, :, :].reshape(n, C)
        pair = jnp.where(core == 0, mine, other)
        grad = jnp.where(core == 0, other, mine)
        normed, _ = normalize(pair.astype(F32))
        x = (normed * gain_ref[...] + shift_ref[...]).astype(BF16)
        wide = dot_nt(w_scr[0:256, :], x)
        q_t = wide[0:64].astype(BF16)
        gate = jax.nn.sigmoid(wide[64:128])
        k_t = wide[128:192].astype(BF16)
        v_t = wide[192:256].astype(BF16)
        dgated = dot_nt(w_scr[256:320, :], grad)
        dob_t = (dgated * gate).astype(BF16)
        for h in range(2):
            hs = slice(h * DH, (h + 1) * DH)
            key = dot_nt(x, w_scr[128 + h * DH : 128 + (h + 1) * DH, :]).astype(BF16)
            value = dot_nt(x, w_scr[192 + h * DH : 192 + (h + 1) * DH, :]).astype(BF16)
            s = dot_nn(key, q_t[hs]) * (scale * LOG2E) + bias_scr[h]
            expo = jnp.exp2(s - jnp.max(s, axis=0, keepdims=True))
            probs = expo * (1.0 / jnp.sum(expo, axis=0, keepdims=True))
            probs_b = probs.astype(BF16)
            o_t = dot_nn(v_t[hs], probs_b)
            dob_h = dob_t[hs]
            delta = jnp.sum(dob_h.astype(F32) * o_t, axis=0, keepdims=True)
            ds = probs * (dot_nn(value, dob_h) - delta)
            acc_scr[h] += ds
            ds_b = ds.astype(BF16)
            dg, ga = dgated[hs], gate[hs]
            d_scr[h * DH : (h + 1) * DH, :] = (dot_nn(k_t[hs], ds_b) * scale).astype(BF16)
            d_scr[64 + h * DH : 64 + (h + 1) * DH, :] = (dg * o_t * ga * (1.0 - ga)).astype(BF16)
            d_scr[128 + h * DH : 128 + (h + 1) * DH, :] = (
                dot_nt(q_t[hs], ds_b) * scale
            ).astype(BF16)
            d_scr[192 + h * DH : 192 + (h + 1) * DH, :] = dot_nt(dob_h, probs_b).astype(BF16)
            gated = (ga * o_t).astype(BF16)
            wacc_scr[256 + h * DH : 256 + (h + 1) * DH, :] += dot_nn(gated, grad)
        d = d_scr[...]
        dx = dot_tn(d, w_scr[0:256, :])
        out_ref[src, 0:cols, :] = dx.astype(BF16).reshape(blocks, cols, C)
        wacc_scr[0:256, :] += dot_nn(d, x)
        return carry

    lax.fori_loop(0, groups, one_row, 0)

    for r in range(0, groups, 2):
        sl = slice(r * 64, r * 64 + 128)
        h0, h1 = acc_scr[0, :, sl], acc_scr[1, :, sl]
        b0 = jnp.where(low, h0, pltpu.roll(h1, 64, 1)).astype(BF16)
        b1 = jnp.where(low, pltpu.roll(h0, 64, 1), h1).astype(BF16)
        out_ref[r * blocks : (r + 1) * blocks, cols : 2 * cols, :] = b0.reshape(blocks, cols, C)
        out_ref[(r + 1) * blocks : (r + 2) * blocks, cols : 2 * cols, :] = b1.reshape(
            blocks, cols, C
        )
    for i in range(64):
        part = wacc_scr[5 * i : 5 * i + 8, :]
        high = part.astype(BF16).astype(F32)
        both = jnp.concatenate([high, part - high], axis=0).astype(BF16)
        out_ref[2 * i, 64:80, :] = both
        out_ref[2 * i + 1, 64:80, :] = both


def owner_kernel(
    core_ref, got_ref, pair_ref, xt_ref, gain_ref, wb_ref,
    dpair_ref, sums_ref, z_scr, dxb_scr, wb_scr, s_scr,
):
    core = core_ref[0]
    rows, cols = pair_ref.shape[0], pair_ref.shape[1]
    z_scr[...] = jnp.zeros_like(z_scr)
    wb_scr[...] = jnp.zeros_like(wb_scr)
    wb_scr[0:4, :] = wb_ref[...].astype(F32)
    for pair in range(2):

        def add(i, total, pair=pair):
            return total + got_ref[i, pair, cols : 2 * cols, :].astype(F32)

        total = lax.fori_loop(0, rows, add, jnp.zeros((cols, C), F32), unroll=8)
        for k in range(cols):
            for h in range(2):
                z_scr[2 * pair + h : 2 * pair + h + 1, k * rows : (k + 1) * rows] = total[
                    k : k + 1, h * 64 : (h + 1) * 64
                ]
    z = z_scr[...].astype(BF16)
    dxb_scr[...] = dot_tn(z, wb_scr[...].astype(BF16))
    dwb = dot_nn(z, xt_ref[...])

    def add_w(i, total):
        return total + got_ref[i, core, 64:80, :].astype(F32)

    w = lax.fori_loop(0, rows, add_w, jnp.zeros((16, C), F32), unroll=8)
    gain = gain_ref[...]

    def one(i, carry):
        dgain, dshift = carry
        normed, rstd = normalize(pair_ref[i].astype(F32))
        dx = got_ref[i, 0, 0:cols, :].astype(F32) + got_ref[i, 1, 0:cols, :].astype(F32)
        dx = dx + dxb_scr[pl.ds(i, cols, stride=rows), :]
        dn = dx * gain
        out = rstd * (
            dn
            - jnp.mean(dn, axis=-1, keepdims=True)
            - normed * jnp.mean(dn * normed, axis=-1, keepdims=True)
        )
        dpair_ref[i] = out.astype(BF16)
        return dgain + dx * normed, dshift + dx

    zero = jnp.zeros((cols, C), F32)
    dgain, dshift = lax.fori_loop(0, rows, one, (zero, zero), unroll=8)
    dgain = jnp.sum(dgain, axis=0, keepdims=True)
    dshift = jnp.sum(dshift, axis=0, keepdims=True)
    s_scr[0:8, :] = w[0:8] + w[8:16]
    s_scr[8:12, :] = dwb[0:4]
    s_scr[12:13, :] = dgain
    s_scr[13:14, :] = dshift
    s_scr[14:15, :] = dgain - dgain.astype(BF16).astype(F32)
    s_scr[15:16, :] = dshift - dshift.astype(BF16).astype(F32)
    sums_ref[...] = jnp.broadcast_to(s_scr[...].astype(BF16)[None], sums_ref.shape)


def final_kernel(
    got_ref, dgain_ref, dshift_ref, dq_ref, dk_ref, dv_ref, dg_ref, db_ref, do_ref, w_scr
):
    chips = got_ref.shape[0]
    zero = jnp.zeros((16, C), F32)

    def add(i, total):
        return total + (got_ref[i, 0].astype(F32) + got_ref[i, 1].astype(F32))

    total = lax.fori_loop(0, chips, add, zero, unroll=8)
    db_ref[...] = total[8:12]
    dgain_ref[...] = total[12:13] + total[14:15]
    dshift_ref[...] = total[13:14] + total[15:16]
    for core in range(2):
        for i in range(chips):
            w_scr[core, 5 * i : 5 * i + 8, :] = got_ref[i, core].astype(F32)[0:8]
    for slot, ref in enumerate((dq_ref, dg_ref, dk_ref, dv_ref)):
        sl = slice(slot * 64, (slot + 1) * 64)
        both = jnp.concatenate([w_scr[0, sl, :], w_scr[1, sl, :]], axis=0)
        ref[...] = jnp.transpose(both)
    do_ref[0:64, :] = w_scr[0, 256:320, :]
    do_ref[64:128, :] = w_scr[1, 256:320, :]


def on_device(
    pair, grad_out, norm_gain, norm_shift, w_query, w_key, w_value, w_gate, w_bias, w_out
):
    axes = ("row", "col")
    rows, cols = pair.shape[0], pair.shape[1]
    devices = 2 * rows
    sds = jax.ShapeDtypeStruct
    gain, shift = norm_gain.reshape(1, C), norm_shift.reshape(1, C)
    wb = w_bias.T
    core = (lax.axis_index("col") % 2).astype(jnp.int32).reshape(1)

    packed, xt = call(
        pack_kernel,
        (sds((rows, 2, 64, C), BF16), sds((rows * cols, C), BF16)),
        5,
        (pltpu.VMEM((rows * cols, C), F32), pltpu.VMEM((cols, C), F32)),
    )(pair, grad_out, gain, shift, wb)
    mine = lax.all_to_all(packed.reshape(devices, 64, C), axes, 0, 0, tiled=True)
    swap = [(i, i ^ 1) for i in range(16)]
    other = lax.ppermute(mine[:, 0:cols, :], "col", swap)
    terms = call(
        attend_kernel,
        sds((devices, 80, C), BF16),
        9,
        (
            pltpu.VMEM((2, 512, 512), F32),
            pltpu.VMEM((2, 512, 512), F32),
            pltpu.VMEM((320, C), BF16),
            pltpu.VMEM((328, C), F32),
            pltpu.VMEM((256, 512), BF16),
        ),
        smem=1,
    )(core, mine, other, gain, shift, w_query, w_key, w_value, w_gate, w_out)
    got = lax.all_to_all(terms, axes, 0, 0, tiled=True).reshape(rows, 2, 80, C)
    d_pair, sums = call(
        owner_kernel,
        (sds(pair.shape, BF16), sds((devices, 16, C), BF16)),
        5,
        (
            pltpu.VMEM((8, rows * cols), F32),
            pltpu.VMEM((rows * cols, C), F32),
            pltpu.VMEM((8, C), F32),
            pltpu.VMEM((16, C), F32),
        ),
        smem=1,
    )(core, got, pair, xt, gain, wb)
    all_sums = lax.all_to_all(sums, axes, 0, 0, tiled=True).reshape(rows, 2, 16, C)
    square = sds((C, C), F32)
    d_gain, d_shift, d_query, d_key, d_value, d_gate, d_bias, d_out = call(
        final_kernel,
        (sds((1, C), F32), sds((1, C), F32), square, square, square, square, sds((H, C), F32), square),
        1,
        (pltpu.VMEM((2, 328, C), F32),),
    )(all_sums)
    return (
        d_pair,
        d_gain.reshape(C),
        d_shift.reshape(C),
        d_query,
        d_key,
        d_value,
        d_gate,
        d_bias.T,
        d_out,
    )


def solution(mesh):
    return jax.shard_map(
        on_device,
        mesh=mesh,
        in_specs=(P("row", "col", None), P("row", "col", None)) + (P(),) * 8,
        out_specs=(P("row", "col", None),) + (P(),) * 8,
        check_vma=False,
    )
```

```python
import jax
import jax.numpy as jnp
from jax import lax
from jax.experimental import pallas as pl
from jax.experimental.pallas import tpu as pltpu
from jax.sharding import PartitionSpec as P

H = 4
DH = 32
C = 128
EPS = 1e-05
LOG2E = 1.4426950408889634
F32 = jnp.float32
BF16 = jnp.bfloat16
MIB = 1024 * 1024


def dot_nn(a, b):
    return lax.dot_general(a, b, (((1,), (0,)), ((), ())), preferred_element_type=F32)


def dot_nt(a, b):
    return lax.dot_general(a, b, (((1,), (1,)), ((), ())), preferred_element_type=F32)


def dot_tn(a, b):
    return lax.dot_general(a, b, (((0,), (0,)), ((), ())), preferred_element_type=F32)


def normalize(values):
    center = values - jnp.mean(values, axis=-1, keepdims=True)
    rstd = lax.rsqrt(jnp.mean(center * center, axis=-1, keepdims=True) + EPS)
    return center * rstd, rstd


def call(kernel, out_shape, n_in, scratch=(), smem=0, vmem=16, flops=0, moved=0):
    specs = [pl.BlockSpec(memory_space=pltpu.SMEM)] * smem
    specs += [pl.BlockSpec(memory_space=pltpu.VMEM)] * n_in
    outs = jax.tree.map(lambda _: pl.BlockSpec(memory_space=pltpu.VMEM), out_shape)
    return pl.pallas_call(
        kernel,
        out_shape=out_shape,
        in_specs=specs,
        out_specs=outs,
        scratch_shapes=list(scratch),
        cost_estimate=pl.CostEstimate(flops=flops, bytes_accessed=moved, transcendentals=0),
        compiler_params=pltpu.CompilerParams(vmem_limit_bytes=vmem * MIB),
    )


def pack_kernel(
    pair_ref, grad_ref, gain_ref, shift_ref, wb_ref, out_ref, xt_ref, nt_ref, n_scr, b_scr
):
    rows, cols = pair_ref.shape[0], pair_ref.shape[1]
    out_ref[:, 0, 0:cols, :] = pair_ref[...]
    out_ref[:, 1, 0:cols, :] = grad_ref[...]
    normed, _ = normalize(pair_ref[...].reshape(rows * cols, C).astype(F32))
    n_scr[...] = normed
    for k in range(cols):
        part = n_scr[pl.ds(k, rows, stride=cols), :]
        nt_ref[k * rows : (k + 1) * rows, :] = part.astype(BF16)
        xt_ref[k * rows : (k + 1) * rows, :] = (part * gain_ref[...] + shift_ref[...]).astype(BF16)
    bias = dot_nt(wb_ref[...], xt_ref[...])
    for pair in range(2):
        for k in range(cols):
            part = bias[2 * pair : 2 * pair + 2, k * rows : (k + 1) * rows]
            b_scr[k : k + 1, :] = jnp.concatenate([part[0:1], part[1:2]], axis=1)
        packed = b_scr[...].astype(BF16)
        out_ref[:, pair, cols : 2 * cols, :] = jnp.broadcast_to(packed[None], (rows, cols, C))


def attend_kernel(
    core_ref, mine_ref, other_ref, gain_ref, shift_ref, wq_ref, wk_ref, wv_ref, wg_ref, wo_ref,
    out_ref, norm_ref, bias_scr, acc_scr, w_scr, wacc_scr, d_scr, rhs_scr,
):
    core = core_ref[0]
    groups, blocks, cols, step_rows = 8, 16, 32, 2
    n = blocks * cols
    scale = DH ** (-0.5)
    lane = lax.broadcasted_iota(jnp.int32, (n, C), 1)
    low = lane < 64

    for slot, ref in enumerate((wq_ref, wg_ref, wk_ref, wv_ref)):
        turned = jnp.transpose(ref[...].astype(F32)).astype(BF16)
        w_scr[slot * 64 : (slot + 1) * 64, :] = jnp.where(core == 0, turned[0:64], turned[64:128])
    w_scr[256:320, :] = jnp.where(core == 0, wo_ref[0:64, :], wo_ref[64:128, :])

    for r in range(0, groups, 2):
        b0 = mine_ref[r * blocks : (r + 1) * blocks, cols : 2 * cols, :].reshape(n, C).astype(F32)
        b1 = mine_ref[(r + 1) * blocks : (r + 2) * blocks, cols : 2 * cols, :].reshape(n, C)
        b1 = b1.astype(F32)
        sl = slice(r * 64, r * 64 + 128)
        bias_scr[0, :, sl] = jnp.where(low, b0, pltpu.roll(b1, 64, 1)) * LOG2E
        bias_scr[1, :, sl] = jnp.where(low, pltpu.roll(b0, 64, 1), b1) * LOG2E
    acc_scr[...] = jnp.zeros_like(acc_scr)
    wacc_scr[...] = jnp.zeros_like(wacc_scr)
    rhs_scr[...] = jnp.zeros_like(rhs_scr)
    norm_ref[...] = jnp.zeros_like(norm_ref)

    def some_rows(it, carry):
        held, items = [], []
        for a in range(step_rows):
            src = pl.ds((it * step_rows + a) * blocks, blocks)
            mine = mine_ref[src, 0:cols, :].reshape(n, C)
            other = other_ref[src, :, :].reshape(n, C)
            pair = jnp.where(core == 0, mine, other)
            grad = jnp.where(core == 0, other, mine)
            normed, _ = normalize(pair.astype(F32))
            x = (normed * gain_ref[...] + shift_ref[...]).astype(BF16)
            wide = dot_nt(w_scr[0:256, :], x)
            q_t = wide[0:64].astype(BF16)
            gate = jax.nn.sigmoid(wide[64:128])
            k_t = wide[128:192].astype(BF16)
            v_t = wide[192:256].astype(BF16)
            dgated = dot_nt(w_scr[256:320, :], grad)
            dob_t = (dgated * gate).astype(BF16)
            kv = dot_nt(x, w_scr[128:256, :]).astype(BF16)
            row = dict(src=src, x=x, normed=normed, grad=grad, gate=gate, dgated=dgated, o=[])
            held.append(row)
            for h in range(2):
                hs = slice(h * DH, (h + 1) * DH)
                slot = 4 * a + 2 * h
                rhs_scr[slot, hs, :] = q_t[hs]
                rhs_scr[slot + 1, 64 + h * DH : 64 + (h + 1) * DH, :] = dob_t[hs]
                items.append(
                    dict(a=a, h=h, slot=slot, kv=kv, q=q_t[hs], k=k_t[hs], v=v_t[hs], dob=dob_t[hs])
                )

        def score(t):
            t["s"] = dot_nn(t["kv"], rhs_scr[t["slot"]]) * (scale * LOG2E) + bias_scr[t["h"]]

        def soften(t):
            expo = jnp.exp2(t["s"] - jnp.max(t["s"], axis=0, keepdims=True))
            t["p"] = expo * (1.0 / jnp.sum(expo, axis=0, keepdims=True))
            t["pb"] = t["p"].astype(BF16)

        def apply(t):
            t["o"] = dot_nn(t["v"], t["pb"])
            t["dp"] = dot_nn(t["kv"], rhs_scr[t["slot"] + 1])

        def back(t):
            delta = jnp.sum(t["dob"].astype(F32) * t["o"], axis=0, keepdims=True)
            t["ds"] = t["p"] * (t["dp"] - delta)
            t["dsb"] = t["ds"].astype(BF16)
            t["dv"] = dot_nt(t["dob"], t["pb"])

        def spread(t):
            h, base = t["h"], 256 * t["a"]
            dq = dot_nn(t["k"], t["dsb"]) * scale
            dk = dot_nt(t["q"], t["dsb"]) * scale
            d_scr[base + h * DH : base + (h + 1) * DH, :] = dq.astype(BF16)
            d_scr[base + 128 + h * DH : base + 128 + (h + 1) * DH, :] = dk.astype(BF16)
            d_scr[base + 192 + h * DH : base + 192 + (h + 1) * DH, :] = t["dv"].astype(BF16)

        stages = (score, soften, apply, back, spread)
        for time in range(len(items) + len(stages) - 1):
            for place, t in enumerate(items):
                if 0 <= time - place < len(stages):
                    stages[time - place](t)
        for h in range(2):
            acc_scr[h] += sum(t["ds"] for t in items[1:] if t["h"] == h and t["a"]) + items[h]["ds"]
        for a, row in enumerate(held):
            base = 256 * a
            o_t = jnp.concatenate([items[2 * a]["o"], items[2 * a + 1]["o"]], axis=0)
            gate = row["gate"]
            d_scr[base + 64 : base + 128, :] = (
                row["dgated"] * o_t * gate * (1.0 - gate)
            ).astype(BF16)
            wacc_scr[256:320, :] += dot_nn((gate * o_t).astype(BF16), row["grad"])
            d = d_scr[base : base + 256, :]
            dx = dot_tn(d, w_scr[0:256, :])
            out_ref[row["src"], 0:cols, :] = dx.astype(BF16).reshape(blocks, cols, C)
            wacc_scr[0:256, :] += dot_nn(d, row["x"])
            norm_ref[0:8, :] += jnp.sum((dx * row["normed"]).reshape(64, 8, C), axis=0)
            norm_ref[8:16, :] += jnp.sum(dx.reshape(64, 8, C), axis=0)
        return carry

    lax.fori_loop(0, groups // step_rows, some_rows, 0)

    for r in range(0, groups, 2):
        sl = slice(r * 64, r * 64 + 128)
        h0, h1 = acc_scr[0, :, sl], acc_scr[1, :, sl]
        b0 = jnp.where(low, h0, pltpu.roll(h1, 64, 1)).astype(BF16)
        b1 = jnp.where(low, pltpu.roll(h0, 64, 1), h1).astype(BF16)
        out_ref[r * blocks : (r + 1) * blocks, cols : 2 * cols, :] = b0.reshape(blocks, cols, C)
        out_ref[(r + 1) * blocks : (r + 2) * blocks, cols : 2 * cols, :] = b1.reshape(
            blocks, cols, C
        )
    for i in range(64):
        part = wacc_scr[5 * i : 5 * i + 8, :].astype(BF16)
        out_ref[2 * i, 64:72, :] = part
        out_ref[2 * i + 1, 64:72, :] = part


def sums_kernel(
    core_ref, got_ref, xt_ref, nt_ref, norm_ref, wb_ref, z_ref, sums_ref, z_scr, s_scr
):
    core = core_ref[0]
    rows, cols = got_ref.shape[0], 32
    z_scr[...] = jnp.zeros_like(z_scr)
    for pair in range(2):

        def add(i, total, pair=pair):
            return total + got_ref[i, pair, cols : 2 * cols, :].astype(F32)

        total = lax.fori_loop(0, rows, add, jnp.zeros((cols, C), F32), unroll=8)
        for k in range(cols):
            for h in range(2):
                z_scr[2 * pair + h : 2 * pair + h + 1, k * rows : (k + 1) * rows] = total[
                    k : k + 1, h * 64 : (h + 1) * 64
                ]
    z = z_scr[...].astype(BF16)
    z_ref[...] = z
    dwb = dot_nn(z, xt_ref[...])
    dgn = dot_nn(z, nt_ref[...])

    def add_w(i, total):
        return total + got_ref[i, core, 64:72, :].astype(F32)

    s_scr[0:8, :] = lax.fori_loop(0, rows, add_w, jnp.zeros((8, C), F32), unroll=8)
    s_scr[8:12, :] = dwb[0:4]
    wb = wb_ref[...].astype(F32)
    dgain = jnp.sum(norm_ref[0:8, :], axis=0, keepdims=True)
    dgain = dgain + jnp.sum(dgn[0:4] * wb, axis=0, keepdims=True)
    dshift = jnp.sum(norm_ref[8:16, :], axis=0, keepdims=True)
    total = jnp.sum(z_scr[0:4, :], axis=1, keepdims=True)
    dshift = dshift + jnp.sum(total * wb, axis=0, keepdims=True)
    s_scr[12:13, :] = dgain
    s_scr[13:14, :] = dshift
    s_scr[14:15, :] = dgain - dgain.astype(BF16).astype(F32)
    s_scr[15:16, :] = dshift - dshift.astype(BF16).astype(F32)
    sums_ref[...] = jnp.broadcast_to(s_scr[...].astype(BF16)[None], sums_ref.shape)


def owner_kernel(got_ref, z_ref, pair_ref, gain_ref, wb_ref, dpair_ref, dxb_scr, wb_scr):
    rows, cols = pair_ref.shape[0], pair_ref.shape[1]
    wb_scr[...] = jnp.zeros_like(wb_scr)
    wb_scr[0:4, :] = wb_ref[...].astype(F32)
    dxb_scr[...] = dot_tn(z_ref[...], wb_scr[...].astype(BF16))
    gain = gain_ref[...]

    def some(it, carry):
        i0 = it * 8
        normed, rstd = normalize(pair_ref[pl.ds(i0, 8)].astype(F32))
        dx = got_ref[pl.ds(i0, 8), 0, 0:cols, :].astype(F32)
        dx = dx + got_ref[pl.ds(i0, 8), 1, 0:cols, :].astype(F32)
        parts = [dxb_scr[pl.ds(i0 + u, cols, stride=rows), :][None] for u in range(8)]
        dn = (dx + jnp.concatenate(parts, axis=0)) * gain
        out = rstd * (
            dn
            - jnp.mean(dn, axis=-1, keepdims=True)
            - normed * jnp.mean(dn * normed, axis=-1, keepdims=True)
        )
        dpair_ref[pl.ds(i0, 8)] = out.astype(BF16)
        return carry

    lax.fori_loop(0, rows // 8, some, 0)


def final_kernel(
    got_ref, dgain_ref, dshift_ref, dq_ref, dk_ref, dv_ref, dg_ref, db_ref, do_ref, w_scr
):
    chips = got_ref.shape[0]
    zero = jnp.zeros((16, C), F32)

    def add(i, total):
        return total + (got_ref[i, 0].astype(F32) + got_ref[i, 1].astype(F32))

    total = lax.fori_loop(0, chips, add, zero, unroll=8)
    db_ref[...] = total[8:12]
    dgain_ref[...] = total[12:13] + total[14:15]
    dshift_ref[...] = total[13:14] + total[15:16]
    for core in range(2):
        for i in range(chips):
            w_scr[core, 5 * i : 5 * i + 8, :] = got_ref[i, core].astype(F32)[0:8]
    for slot, ref in enumerate((dq_ref, dg_ref, dk_ref, dv_ref)):
        sl = slice(slot * 64, (slot + 1) * 64)
        both = jnp.concatenate([w_scr[0, sl, :], w_scr[1, sl, :]], axis=0)
        ref[...] = jnp.transpose(both)
    do_ref[0:64, :] = w_scr[0, 256:320, :]
    do_ref[64:128, :] = w_scr[1, 256:320, :]


def on_device(
    pair, grad_out, norm_gain, norm_shift, w_query, w_key, w_value, w_gate, w_bias, w_out
):
    axes = ("row", "col")
    rows, cols = pair.shape[0], pair.shape[1]
    devices = 2 * rows
    sds = jax.ShapeDtypeStruct
    gain, shift = norm_gain.reshape(1, C), norm_shift.reshape(1, C)
    wb = w_bias.T
    core = (lax.axis_index("col") % 2).astype(jnp.int32).reshape(1)

    turned = sds((rows * cols, C), BF16)
    packed, xt, nt = call(
        pack_kernel,
        (sds((rows, 2, 64, C), BF16), turned, turned),
        5,
        (pltpu.VMEM((rows * cols, C), F32), pltpu.VMEM((cols, C), F32)),
        flops=10**8,
        moved=4 * MIB,
    )(pair, grad_out, gain, shift, wb)
    mine = lax.all_to_all(packed.reshape(devices, 64, C), axes, 0, 0, tiled=True)
    swap = [(i, i ^ 1) for i in range(16)]
    other = lax.ppermute(mine[:, 0:cols, :], "col", swap)
    terms, norms = call(
        attend_kernel,
        (sds((devices, 72, C), BF16), sds((16, C), F32)),
        9,
        (
            pltpu.VMEM((2, 512, 512), F32),
            pltpu.VMEM((2, 512, 512), F32),
            pltpu.VMEM((320, C), BF16),
            pltpu.VMEM((328, C), F32),
            pltpu.VMEM((512, 512), BF16),
            pltpu.VMEM((8, C, 512), BF16),
        ),
        smem=1,
        vmem=32,
        flops=10**10,
        moved=6 * MIB,
    )(core, mine, other, gain, shift, w_query, w_key, w_value, w_gate, w_out)
    got = lax.all_to_all(terms, axes, 0, 0, tiled=True).reshape(rows, 2, 72, C)
    z, sums = call(
        sums_kernel,
        (sds((8, rows * cols), BF16), sds((devices, 16, C), BF16)),
        5,
        (pltpu.VMEM((8, rows * cols), F32), pltpu.VMEM((16, C), F32)),
        smem=1,
        flops=10**8,
        moved=4 * MIB,
    )(core, got, xt, nt, norms, wb)
    all_sums = lax.all_to_all(sums, axes, 0, 0, tiled=True).reshape(rows, 2, 16, C)
    d_pair = call(
        owner_kernel,
        sds(pair.shape, BF16),
        5,
        (pltpu.VMEM((rows * cols, C), F32), pltpu.VMEM((8, C), F32)),
        flops=10**8,
        moved=8 * MIB,
    )(got, z, pair, gain, wb)
    square = sds((C, C), F32)
    d_gain, d_shift, d_query, d_key, d_value, d_gate, d_bias, d_out = call(
        final_kernel,
        (sds((1, C), F32), sds((1, C), F32), square, square, square, square, sds((H, C), F32), square),
        1,
        (pltpu.VMEM((2, 328, C), F32),),
        moved=MIB,
    )(all_sums)
    return (
        d_pair,
        d_gain.reshape(C),
        d_shift.reshape(C),
        d_query,
        d_key,
        d_value,
        d_gate,
        d_bias.T,
        d_out,
    )


def solution(mesh):
    return jax.shard_map(
        on_device,
        mesh=mesh,
        in_specs=(P("row", "col", None), P("row", "col", None)) + (P(),) * 8,
        out_specs=(P("row", "col", None),) + (P(),) * 8,
        check_vma=False,
    )
```

```python
import jax
import jax.numpy as jnp
from jax import lax
from jax.experimental import pallas as pl
from jax.experimental.pallas import tpu as pltpu
from jax.sharding import PartitionSpec as P

H = 4
DH = 32
C = 128
EPS = 1e-05
LOG2E = 1.4426950408889634
F32 = jnp.float32
BF16 = jnp.bfloat16
MIB = 1024 * 1024


def dot_nn(a, b):
    return lax.dot_general(a, b, (((1,), (0,)), ((), ())), preferred_element_type=F32)


def dot_nt(a, b):
    return lax.dot_general(a, b, (((1,), (1,)), ((), ())), preferred_element_type=F32)


def dot_tn(a, b):
    return lax.dot_general(a, b, (((0,), (0,)), ((), ())), preferred_element_type=F32)


def normalize(values):
    center = values - jnp.mean(values, axis=-1, keepdims=True)
    rstd = lax.rsqrt(jnp.mean(center * center, axis=-1, keepdims=True) + EPS)
    return center * rstd, rstd


def call(
    kernel, out_shape, n_in, scratch=(), smem=0, hbm=0, to_hbm=(), vmem=16, flops=0, moved=0
):
    specs = [pl.BlockSpec(memory_space=pltpu.SMEM)] * smem
    specs += [pl.BlockSpec(memory_space=pltpu.HBM)] * hbm
    specs += [pl.BlockSpec(memory_space=pltpu.VMEM)] * n_in
    many = isinstance(out_shape, tuple)
    shapes = out_shape if many else (out_shape,)
    spaces = [pltpu.HBM if i in to_hbm else pltpu.VMEM for i in range(len(shapes))]
    outs = [pl.BlockSpec(memory_space=space) for space in spaces]
    outs = tuple(outs) if many else outs[0]
    return pl.pallas_call(
        kernel,
        out_shape=out_shape,
        in_specs=specs,
        out_specs=outs,
        scratch_shapes=list(scratch),
        cost_estimate=pl.CostEstimate(flops=flops, bytes_accessed=moved, transcendentals=0),
        compiler_params=pltpu.CompilerParams(vmem_limit_bytes=vmem * MIB),
    )


def in_hbm(array):
    return pltpu.with_memory_space_constraint(array, pltpu.HBM)


def pack_kernel(
    pair_hbm, grad_hbm, gain_hbm, shift_hbm, wb_hbm,
    out_ref, xt_ref, nt_ref, n_scr, b_scr, gain_scr, shift_scr, wb_scr, sems,
):
    rows, cols = pair_hbm.shape[0], pair_hbm.shape[1]
    copies = [
        pltpu.make_async_copy(src, dst, sems.at[i])
        for i, (src, dst) in enumerate(
            (
                (pair_hbm, out_ref.at[:, 0, 0:cols, :]),
                (gain_hbm, gain_scr),
                (shift_hbm, shift_scr),
                (wb_hbm, wb_scr),
                (grad_hbm, out_ref.at[:, 1, 0:cols, :]),
            )
        )
    ]
    for copy in copies:
        copy.start()
    for copy in copies[:-1]:
        copy.wait()
    normed, _ = normalize(out_ref[:, 0, 0:cols, :].reshape(rows * cols, C).astype(F32))
    n_scr[...] = normed
    for k in range(cols):
        part = n_scr[pl.ds(k, rows, stride=cols), :]
        nt_ref[k * rows : (k + 1) * rows, :] = part.astype(BF16)
        xt_ref[k * rows : (k + 1) * rows, :] = (part * gain_scr[...] + shift_scr[...]).astype(BF16)
    bias = dot_nt(wb_scr[...], xt_ref[...])
    for pair in range(2):
        for k in range(cols):
            part = bias[2 * pair : 2 * pair + 2, k * rows : (k + 1) * rows]
            b_scr[k : k + 1, :] = jnp.concatenate([part[0:1], part[1:2]], axis=1)
        packed = b_scr[...].astype(BF16)
        out_ref[:, pair, cols : 2 * cols, :] = jnp.broadcast_to(packed[None], (rows, cols, C))
    copies[-1].wait()


def attend_kernel(
    core_ref, mine_ref, other_ref, gain_ref, shift_ref, wq_ref, wk_ref, wv_ref, wg_ref, wo_ref,
    out_hbm, d_hbm, w_scr, bias_scr, acc_scr, wacc_scr, rhs_scr, out_ref, d_ref, sems, d_sems,
):
    core = core_ref[0]
    groups, blocks, cols, step_rows = 8, 16, 32, 4
    n = blocks * cols
    scale = DH ** (-0.5)
    lane = lax.broadcasted_iota(jnp.int32, (n, C), 1)
    low = lane < 64

    for slot, ref in enumerate((wq_ref, wg_ref, wk_ref, wv_ref)):
        turned = jnp.transpose(ref[...].astype(F32)).astype(BF16)
        w_scr[slot * 64 : (slot + 1) * 64, :] = jnp.where(core == 0, turned[0:64], turned[64:128])
    w_scr[256:320, :] = jnp.where(core == 0, wo_ref[0:64, :], wo_ref[64:128, :])

    for r in range(0, groups, 2):
        b0 = mine_ref[r * blocks : (r + 1) * blocks, cols : 2 * cols, :].reshape(n, C).astype(F32)
        b1 = mine_ref[(r + 1) * blocks : (r + 2) * blocks, cols : 2 * cols, :].reshape(n, C)
        b1 = b1.astype(F32)
        sl = slice(r * 64, r * 64 + 128)
        bias_scr[0, :, sl] = jnp.where(low, b0, pltpu.roll(b1, 64, 1)) * LOG2E
        bias_scr[1, :, sl] = jnp.where(low, pltpu.roll(b0, 64, 1), b1) * LOG2E
    acc_scr[...] = jnp.zeros_like(acc_scr)
    wacc_scr[...] = jnp.zeros_like(wacc_scr)
    rhs_scr[...] = jnp.zeros_like(rhs_scr)

    def some_rows(it, carry):
        def prepare(a, row, items):
            src = pl.ds((it * step_rows + a) * blocks, blocks)
            mine = mine_ref[src, 0:cols, :].reshape(n, C)
            other = other_ref[src, :, :].reshape(n, C)
            pair = jnp.where(core == 0, mine, other)
            grad = jnp.where(core == 0, other, mine)
            normed, _ = normalize(pair.astype(F32))
            x = (normed * gain_ref[...] + shift_ref[...]).astype(BF16)
            wide = dot_nt(w_scr[0:256, :], x)
            q_t = wide[0:64].astype(BF16)
            gate = jax.nn.sigmoid(wide[64:128])
            k_t = wide[128:192].astype(BF16)
            v_t = wide[192:256].astype(BF16)
            dgated = dot_nt(w_scr[256:320, :], grad)
            dob_t = (dgated * gate).astype(BF16)
            kv = dot_nt(x, w_scr[128:256, :]).astype(BF16)
            row.update(x=x, grad=grad, gate=gate, dgated=dgated)
            for h in range(2):
                hs = slice(h * DH, (h + 1) * DH)
                slot = 4 * a + 2 * h
                rhs_scr[slot, hs, :] = q_t[hs]
                rhs_scr[slot + 1, 64 + h * DH : 64 + (h + 1) * DH, :] = dob_t[hs]
                items[h].update(a=a, h=h, slot=slot, kv=kv)
                items[h].update(q=q_t[hs], k=k_t[hs], v=v_t[hs], dob=dob_t[hs])

        def score(t):
            t["s"] = dot_nn(t["kv"], rhs_scr[t["slot"]]) * (scale * LOG2E) + bias_scr[t["h"]]

        def soften(t):
            expo = jnp.exp2(t["s"] - jnp.max(t["s"], axis=0, keepdims=True))
            t["p"] = expo * (1.0 / jnp.sum(expo, axis=0, keepdims=True))
            t["pb"] = t["p"].astype(BF16)

        def apply(t):
            t["o"] = dot_nn(t["v"], t["pb"])
            t["dp"] = dot_nn(t["kv"], rhs_scr[t["slot"] + 1])

        def back(t):
            delta = jnp.sum(t["dob"].astype(F32) * t["o"], axis=0, keepdims=True)
            ds = t["p"] * (t["dp"] - delta)
            t["dsb"] = ds.astype(BF16)
            t["dv"] = dot_nt(t["dob"], t["pb"])
            acc_scr[t["h"]] += ds

        def spread(t):
            h, here = t["h"], it * step_rows + t["a"]
            dq = dot_nn(t["k"], t["dsb"]) * scale
            dk = dot_nt(t["q"], t["dsb"]) * scale
            d_ref[here, h * DH : (h + 1) * DH, :] = dq.astype(BF16)
            d_ref[here, 128 + h * DH : 128 + (h + 1) * DH, :] = dk.astype(BF16)
            d_ref[here, 192 + h * DH : 192 + (h + 1) * DH, :] = t["dv"].astype(BF16)

        def finish(a, row, items):
            here = it * step_rows + a
            o_t = jnp.concatenate([items[0]["o"], items[1]["o"]], axis=0)
            gate = row["gate"]
            d_ref[here, 64:128, :] = (
                row["dgated"] * o_t * gate * (1.0 - gate)
            ).astype(BF16)
            wacc_scr[256:320, :] += dot_nn((gate * o_t).astype(BF16), row["grad"])
            pltpu.make_async_copy(d_ref.at[here], d_hbm.at[here], d_sems.at[here]).start()
            wacc_scr[0:256, :] += dot_nn(d_ref[here], row["x"])

        def both(t):
            apply(t)
            back(t)

        stages = (score, soften, both, spread)
        depth = len(stages)
        plan = []
        for a in range(step_rows):
            row, items = {}, ({}, {})
            ready = lambda a=a, row=row, items=items: prepare(a, row, items)
            plan.append((2 * a - 1, 0, ready))
            for h in range(2):
                for place, stage in enumerate(stages):
                    when = 2 * a + h + place
                    plan.append((when, 1 + 2 * a + h, lambda stage=stage, t=items[h]: stage(t)))
            done = lambda a=a, row=row, items=items: finish(a, row, items)
            plan.append((2 * a + depth, 2 * a + 2.5, done))
        for _, _, act in sorted(plan, key=lambda e: (e[0], e[1])):
            act()
        return carry

    lax.fori_loop(0, groups // step_rows, some_rows, 0)

    for i in range(64):
        part = wacc_scr[5 * i : 5 * i + 8, :].astype(BF16)
        out_ref[2 * i, cols : cols + 8, :] = part
        out_ref[2 * i + 1, cols : cols + 8, :] = part
    copies = []
    for r in range(0, groups, 2):
        sl = slice(r * 64, r * 64 + 128)
        h0, h1 = acc_scr[0, :, sl], acc_scr[1, :, sl]
        b0 = jnp.where(low, h0, pltpu.roll(h1, 64, 1)).astype(BF16)
        b1 = jnp.where(low, pltpu.roll(h0, 64, 1), h1).astype(BF16)
        out_ref[r * blocks : (r + 1) * blocks, 0:cols, :] = b0.reshape(blocks, cols, C)
        out_ref[(r + 1) * blocks : (r + 2) * blocks, 0:cols, :] = b1.reshape(blocks, cols, C)
        part = pl.ds(r * blocks, 2 * blocks)
        copies.append(pltpu.make_async_copy(out_ref.at[part], out_hbm.at[part], sems.at[r // 2]))
        copies[-1].start()
    for r in range(groups):
        copies.append(pltpu.make_async_copy(d_ref.at[r], d_hbm.at[r], d_sems.at[r]))
    for copy in copies:
        copy.wait()


def dx_kernel(core_ref, mine_ref, other_ref, d_ref, w_ref, keep_ref, send_ref, norm_ref):
    core = core_ref[0]
    groups, blocks, cols = 8, 16, 32
    n, half = blocks * cols, cols // 2
    norm_ref[...] = jnp.zeros_like(norm_ref)

    def one_row(r, carry):
        src = pl.ds(r * blocks, blocks)
        mine = mine_ref[src, 0:cols, :].reshape(n, C)
        pair = jnp.where(core == 0, mine, other_ref[src, :, :].reshape(n, C))
        normed, _ = normalize(pair.astype(F32))
        dx = dot_tn(d_ref[r], w_ref[0:256, :])
        norm_ref[0:8, :] += jnp.sum((dx * normed).reshape(n // 8, 8, C), axis=0)
        norm_ref[8:16, :] += jnp.sum(dx.reshape(n // 8, 8, C), axis=0)
        dx = dx.astype(BF16).reshape(blocks, cols, C)
        keep_ref[src] = jnp.where(core == 0, dx[:, 0:half], dx[:, half:cols])
        send_ref[src] = jnp.where(core == 0, dx[:, half:cols], dx[:, 0:half])
        return carry

    lax.fori_loop(0, groups, one_row, 0, unroll=2)


def sums_kernel(
    core_ref, both_hbm, xt_hbm, nt_hbm, got_ref, norm_ref, wb_ref,
    z_ref, sums_hbm, z_scr, s_scr, sums_ref, xt_ref, nt_ref, sems,
):
    core = core_ref[0]
    rows, cols = got_ref.shape[0], 32
    copies = [
        pltpu.make_async_copy(xt_hbm, xt_ref, sems.at[0]),
        pltpu.make_async_copy(nt_hbm, nt_ref, sems.at[1]),
        pltpu.make_async_copy(both_hbm, sums_ref.at[:, 16:32, :], sems.at[2]),
    ]
    for copy in copies:
        copy.start()
    z_scr[...] = jnp.zeros_like(z_scr)
    for pair in range(2):

        def add(i, total, pair=pair):
            return total + got_ref[i, pair, 0:cols, :].astype(F32)

        total = lax.fori_loop(0, rows, add, jnp.zeros((cols, C), F32), unroll=8)
        for k in range(cols):
            for h in range(2):
                z_scr[2 * pair + h : 2 * pair + h + 1, k * rows : (k + 1) * rows] = total[
                    k : k + 1, h * 64 : (h + 1) * 64
                ]
    z = z_scr[...].astype(BF16)
    z_ref[...] = z
    copies[2].wait()
    last = pltpu.make_async_copy(sums_ref.at[:, 16:32, :], sums_hbm.at[:, 16:32, :], sems.at[3])
    last.start()
    copies[0].wait()
    copies[1].wait()
    dwb = dot_nn(z, xt_ref[...])
    dgn = dot_nn(z, nt_ref[...])

    def add_w(i, total):
        return total + got_ref[i, core, cols : cols + 8, :].astype(F32)

    s_scr[0:8, :] = lax.fori_loop(0, rows, add_w, jnp.zeros((8, C), F32), unroll=8)
    s_scr[8:12, :] = dwb[0:4]
    wb = wb_ref[...].astype(F32)
    dgain = jnp.sum(norm_ref[0:8, :], axis=0, keepdims=True)
    dgain = dgain + jnp.sum(dgn[0:4] * wb, axis=0, keepdims=True)
    dshift = jnp.sum(norm_ref[8:16, :], axis=0, keepdims=True)
    total = jnp.sum(z_scr[0:4, :], axis=1, keepdims=True)
    dshift = dshift + jnp.sum(total * wb, axis=0, keepdims=True)
    s_scr[12:13, :] = dgain
    s_scr[13:14, :] = dshift
    s_scr[14:15, :] = dgain - dgain.astype(BF16).astype(F32)
    s_scr[15:16, :] = dshift - dshift.astype(BF16).astype(F32)
    sums_ref[:, 0:16, :] = jnp.broadcast_to(s_scr[...].astype(BF16)[None], (2 * rows, 16, C))
    first = pltpu.make_async_copy(sums_ref.at[:, 0:16, :], sums_hbm.at[:, 0:16, :], sems.at[4])
    first.start()
    last.wait()
    first.wait()


def ready_kernel(
    z_ref, pair_ref, wb_ref, dxb_hbm, normed_hbm, rstd_hbm,
    dxb_scr, wb_scr, dxb_ref, normed_ref, rstd_ref, sems,
):
    rows, cols = pair_ref.shape[0], pair_ref.shape[1]
    wb_scr[...] = jnp.zeros_like(wb_scr)
    wb_scr[0:4, :] = wb_ref[...].astype(F32)
    dxb_scr[...] = dot_tn(z_ref[...], wb_scr[...].astype(BF16))

    def some(it, carry):
        i0 = it * 8
        part = pl.ds(i0, 8)
        normed, rstd = normalize(pair_ref[part].astype(F32))
        normed_ref[part] = normed
        rstd_ref[part] = jnp.broadcast_to(rstd, normed.shape)
        for u in range(8):
            dxb_ref[i0 + u] = dxb_scr[pl.ds(i0 + u, cols, stride=rows), :]
        return carry

    lax.fori_loop(0, rows // 8, some, 0)
    copies = [
        pltpu.make_async_copy(src, dst, sems.at[i])
        for i, (src, dst) in enumerate(
            ((dxb_ref, dxb_hbm), (normed_ref, normed_hbm), (rstd_ref, rstd_hbm))
        )
    ]
    for copy in copies:
        copy.start()
    for copy in copies:
        copy.wait()


def final_kernel(
    dxb_hbm, normed_hbm, rstd_hbm, got_ref, gain_ref,
    dpair_hbm, dgain_ref, dshift_ref, dq_ref, dk_ref, dv_ref, dg_ref, db_ref, do_ref,
    w_scr, dxb_ref, normed_ref, rstd_ref, dpair_ref, sems, out_sems,
):
    chips, cols, parts = got_ref.shape[0], dxb_ref.shape[1], out_sems.shape[0]
    size = chips // parts
    fetched = []
    for p in range(parts):
        part = pl.ds(p * size, size)
        fetched.append(
            [
                pltpu.make_async_copy(src.at[part], dst.at[part], sems.at[i, p])
                for i, (src, dst) in enumerate(
                    ((dxb_hbm, dxb_ref), (normed_hbm, normed_ref), (rstd_hbm, rstd_ref))
                )
            ]
        )
        for copy in fetched[-1]:
            copy.start()
    zero = jnp.zeros((16, C), F32)

    def add(i, total):
        return total + (got_ref[i, 0, 0:16, :].astype(F32) + got_ref[i, 1, 0:16, :].astype(F32))

    total = lax.fori_loop(0, chips, add, zero, unroll=8)
    db_ref[...] = total[8:12]
    dgain_ref[...] = total[12:13] + total[14:15]
    dshift_ref[...] = total[13:14] + total[15:16]
    gain = gain_ref[...]
    sent = []
    for p in range(parts):
        for copy in fetched[p]:
            copy.wait()

        def some(it, carry, p=p):
            part = pl.ds(p * size + it * 8, 8)
            normed, rstd = normed_ref[part], rstd_ref[part]
            dx = jnp.concatenate([got_ref[part, 0, 16:32, :], got_ref[part, 1, 16:32, :]], axis=1)
            dn = (dx.astype(F32) + dxb_ref[part]) * gain
            out = rstd * (
                dn
                - jnp.mean(dn, axis=-1, keepdims=True)
                - normed * jnp.mean(dn * normed, axis=-1, keepdims=True)
            )
            dpair_ref[part] = out.astype(BF16)
            return carry

        lax.fori_loop(0, size // 8, some, 0)
        part = pl.ds(p * size, size)
        sent.append(pltpu.make_async_copy(dpair_ref.at[part], dpair_hbm.at[part], out_sems.at[p]))
        sent[-1].start()
    for core in range(2):
        for i in range(chips):
            w_scr[core, 5 * i : 5 * i + 8, :] = got_ref[i, core, 0:16, :].astype(F32)[0:8]
    for slot, ref in enumerate((dq_ref, dg_ref, dk_ref, dv_ref)):
        sl = slice(slot * 64, (slot + 1) * 64)
        heads = jnp.concatenate([w_scr[0, sl, :], w_scr[1, sl, :]], axis=0)
        ref[...] = jnp.transpose(heads)
    do_ref[0:64, :] = w_scr[0, 256:320, :]
    do_ref[64:128, :] = w_scr[1, 256:320, :]
    for copy in sent:
        copy.wait()


def on_device(
    pair, grad_out, norm_gain, norm_shift, w_query, w_key, w_value, w_gate, w_bias, w_out
):
    axes = ("row", "col")
    rows, cols = pair.shape[0], pair.shape[1]
    devices = 2 * rows
    sds = jax.ShapeDtypeStruct
    gain, shift = norm_gain.reshape(1, C), norm_shift.reshape(1, C)
    wb = w_bias.T
    core = (lax.axis_index("col") % 2).astype(jnp.int32).reshape(1)

    turned = sds((rows * cols, C), BF16)
    turned_scr = pltpu.VMEM((rows * cols, C), BF16)
    packed, xt, nt = call(
        pack_kernel,
        (sds((rows, 2, 64, C), BF16), turned, turned),
        0,
        (
            pltpu.VMEM((rows * cols, C), F32),
            pltpu.VMEM((cols, C), F32),
            pltpu.VMEM((1, C), F32),
            pltpu.VMEM((1, C), F32),
            pltpu.VMEM((H, C), BF16),
            pltpu.SemaphoreType.DMA((5,)),
        ),
        hbm=5,
        flops=10**8,
        moved=4 * MIB,
    )(*(in_hbm(a) for a in (pair, grad_out, gain, shift, wb)))
    mine = lax.all_to_all(packed.reshape(devices, 64, C), axes, 0, 0, tiled=True)
    swap = [(i, i ^ 1) for i in range(16)]
    other = lax.ppermute(mine[:, 0:cols, :], "col", swap)
    terms, spread, turned_w = call(
        attend_kernel,
        (
            pltpu.HBM((devices, 40, C), BF16),
            pltpu.HBM((8, 256, 512), BF16),
            sds((320, C), BF16),
        ),
        9,
        (
            pltpu.VMEM((2, 512, 512), F32),
            pltpu.VMEM((2, 512, 512), F32),
            pltpu.VMEM((328, C), F32),
            pltpu.VMEM((16, C, 512), BF16),
            pltpu.VMEM((devices, 40, C), BF16),
            pltpu.VMEM((8, 256, 512), BF16),
            pltpu.SemaphoreType.DMA((4,)),
            pltpu.SemaphoreType.DMA((8,)),
        ),
        smem=1,
        to_hbm=(0, 1),
        vmem=36,
        flops=10**10,
        moved=6 * MIB,
    )(core, mine, other, gain, shift, w_query, w_key, w_value, w_gate, w_out)
    got = lax.all_to_all(terms, axes, 0, 0, tiled=True).reshape(rows, 2, 40, C)
    halves = sds((devices, cols // 2, C), BF16)
    keep, send, norms = call(
        dx_kernel,
        (halves, halves, sds((16, C), F32)),
        4,
        smem=1,
        flops=10**9,
        moved=6 * MIB,
    )(core, mine, other, spread, turned_w)
    came = lax.ppermute(send, "col", swap)
    both = (keep.astype(F32) + came.astype(F32)).astype(BF16)
    z, sums = call(
        sums_kernel,
        (sds((8, rows * cols), BF16), pltpu.HBM((devices, 32, C), BF16)),
        3,
        (
            pltpu.VMEM((8, rows * cols), F32),
            pltpu.VMEM((16, C), F32),
            pltpu.VMEM((devices, 32, C), BF16),
            turned_scr,
            turned_scr,
            pltpu.SemaphoreType.DMA((5,)),
        ),
        smem=1,
        hbm=3,
        to_hbm=(1,),
        flops=10**8,
        moved=4 * MIB,
    )(core, in_hbm(both), in_hbm(xt), in_hbm(nt), got, norms, wb)
    last = lax.all_to_all(sums, axes, 0, 0, tiled=True).reshape(rows, 2, 32, C)
    tile = pltpu.HBM(pair.shape, F32)
    tile_scr = pltpu.VMEM(pair.shape, F32)
    dxb, normed, rstd = call(
        ready_kernel,
        (tile, tile, tile),
        3,
        (
            pltpu.VMEM((rows * cols, C), F32),
            pltpu.VMEM((8, C), F32),
            tile_scr,
            tile_scr,
            tile_scr,
            pltpu.SemaphoreType.DMA((3,)),
        ),
        to_hbm=(0, 1, 2),
        flops=10**8,
        moved=8 * MIB,
    )(z, pair, wb)
    square = sds((C, C), F32)
    d_pair, d_gain, d_shift, d_query, d_key, d_value, d_gate, d_bias, d_out = call(
        final_kernel,
        (
            pltpu.HBM(pair.shape, BF16),
            sds((1, C), F32),
            sds((1, C), F32),
            square,
            square,
            square,
            square,
            sds((H, C), F32),
            square,
        ),
        2,
        (
            pltpu.VMEM((2, 328, C), F32),
            tile_scr,
            tile_scr,
            tile_scr,
            pltpu.VMEM(pair.shape, BF16),
            pltpu.SemaphoreType.DMA((3, 4)),
            pltpu.SemaphoreType.DMA((4,)),
        ),
        hbm=3,
        to_hbm=(0,),
        moved=8 * MIB,
    )(in_hbm(dxb), in_hbm(normed), in_hbm(rstd), last, gain)
    return (
        d_pair,
        d_gain.reshape(C),
        d_shift.reshape(C),
        d_query,
        d_key,
        d_value,
        d_gate,
        d_bias.T,
        d_out,
    )


def solution(mesh):
    return jax.shard_map(
        on_device,
        mesh=mesh,
        in_specs=(P("row", "col", None), P("row", "col", None)) + (P(),) * 8,
        out_specs=(P("row", "col", None),) + (P(),) * 8,
        check_vma=False,
    )
```

```python
import jax
import jax.numpy as jnp
from jax import lax
from jax.experimental import pallas as pl
from jax.experimental.pallas import tpu as pltpu
from jax.sharding import PartitionSpec as P

H = 4
DH = 32
C = 128
EPS = 1e-05
LOG2E = 1.4426950408889634
F32 = jnp.float32
BF16 = jnp.bfloat16
MIB = 1024 * 1024


def dot_nn(a, b):
    return lax.dot_general(a, b, (((1,), (0,)), ((), ())), preferred_element_type=F32)


def dot_nt(a, b):
    return lax.dot_general(a, b, (((1,), (1,)), ((), ())), preferred_element_type=F32)


def dot_tn(a, b):
    return lax.dot_general(a, b, (((0,), (0,)), ((), ())), preferred_element_type=F32)


def normalize(values):
    center = values - jnp.mean(values, axis=-1, keepdims=True)
    rstd = lax.rsqrt(jnp.mean(center * center, axis=-1, keepdims=True) + EPS)
    return center * rstd, rstd


def mean_lanes(values):
    return dot_nn(values.astype(BF16), jnp.full((C, C), 1.0 / C, BF16))


def call(
    kernel, out_shape, n_in, scratch=(), smem=0, hbm=0, to_hbm=(), vmem=16, flops=0, moved=0
):
    specs = [pl.BlockSpec(memory_space=pltpu.SMEM)] * smem
    specs += [pl.BlockSpec(memory_space=pltpu.HBM)] * hbm
    specs += [pl.BlockSpec(memory_space=pltpu.VMEM)] * n_in
    many = isinstance(out_shape, tuple)
    shapes = out_shape if many else (out_shape,)
    spaces = [pltpu.HBM if i in to_hbm else pltpu.VMEM for i in range(len(shapes))]
    outs = [pl.BlockSpec(memory_space=space) for space in spaces]
    outs = tuple(outs) if many else outs[0]
    return pl.pallas_call(
        kernel,
        out_shape=out_shape,
        in_specs=specs,
        out_specs=outs,
        scratch_shapes=list(scratch),
        cost_estimate=pl.CostEstimate(flops=flops, bytes_accessed=moved, transcendentals=0),
        compiler_params=pltpu.CompilerParams(vmem_limit_bytes=vmem * MIB),
    )


def in_hbm(array):
    return pltpu.with_memory_space_constraint(array, pltpu.HBM)


def pack_kernel(
    pair_hbm, grad_hbm, gain_hbm, shift_hbm, wb_hbm,
    out_ref, nt_ref, n_scr, b_scr, gain_scr, shift_scr, wb_scr, xt_ref, sems,
):
    rows, cols = pair_hbm.shape[0], pair_hbm.shape[1]
    copies = [
        pltpu.make_async_copy(src, dst, sems.at[i])
        for i, (src, dst) in enumerate(
            (
                (pair_hbm, out_ref.at[:, 0, 0:cols, :]),
                (gain_hbm, gain_scr),
                (shift_hbm, shift_scr),
                (wb_hbm, wb_scr),
                (grad_hbm, out_ref.at[:, 1, 0:cols, :]),
            )
        )
    ]
    for copy in copies:
        copy.start()
    for copy in copies[:-1]:
        copy.wait()
    normed, _ = normalize(out_ref[:, 0, 0:cols, :].reshape(rows * cols, C).astype(F32))
    n_scr[...] = normed
    for k in range(cols):
        part = n_scr[pl.ds(k, rows, stride=cols), :]
        nt_ref[k * rows : (k + 1) * rows, :] = part.astype(BF16)
        xt_ref[k * rows : (k + 1) * rows, :] = (part * gain_scr[...] + shift_scr[...]).astype(BF16)
    bias = dot_nt(wb_scr[...], xt_ref[...])
    for pair in range(2):
        for k in range(cols):
            part = bias[2 * pair : 2 * pair + 2, k * rows : (k + 1) * rows]
            b_scr[k : k + 1, :] = jnp.concatenate([part[0:1], part[1:2]], axis=1)
        packed = b_scr[...].astype(BF16)
        out_ref[:, pair, cols : 2 * cols, :] = jnp.broadcast_to(packed[None], (rows, cols, C))
    copies[-1].wait()


def attend_kernel(
    core_ref, mine_ref, other_ref, gain_ref, shift_ref, wq_ref, wk_ref, wv_ref, wg_ref, wo_ref,
    out_hbm, d_hbm, w_scr, bias_scr, acc_scr, wacc_scr, rhs_scr, out_ref, d_ref, sems, d_sems,
):
    core = core_ref[0]
    groups, blocks, cols, step_rows = 8, 16, 32, 4
    n = blocks * cols
    scale = DH ** (-0.5)
    lane = lax.broadcasted_iota(jnp.int32, (n, C), 1)
    low = lane < 64

    for slot, ref in enumerate((wq_ref, wg_ref, wk_ref, wv_ref)):
        turned = jnp.transpose(ref[...].astype(F32)).astype(BF16)
        w_scr[slot * 64 : (slot + 1) * 64, :] = jnp.where(core == 0, turned[0:64], turned[64:128])
    w_scr[256:320, :] = jnp.where(core == 0, wo_ref[0:64, :], wo_ref[64:128, :])

    for r in range(0, groups, 2):
        b0 = mine_ref[r * blocks : (r + 1) * blocks, cols : 2 * cols, :].reshape(n, C).astype(F32)
        b1 = mine_ref[(r + 1) * blocks : (r + 2) * blocks, cols : 2 * cols, :].reshape(n, C)
        b1 = b1.astype(F32)
        sl = slice(r * 64, r * 64 + 128)
        bias_scr[0, :, sl] = jnp.where(low, b0, pltpu.roll(b1, 64, 1)) * LOG2E
        bias_scr[1, :, sl] = jnp.where(low, pltpu.roll(b0, 64, 1), b1) * LOG2E
    acc_scr[...] = jnp.zeros_like(acc_scr)
    wacc_scr[...] = jnp.zeros_like(wacc_scr)
    rhs_scr[...] = jnp.zeros_like(rhs_scr)

    def some_rows(it, carry):
        def prepare(a, row, items):
            src = pl.ds((it * step_rows + a) * blocks, blocks)
            mine = mine_ref[src, 0:cols, :].reshape(n, C)
            other = other_ref[src, :, :].reshape(n, C)
            pair = jnp.where(core == 0, mine, other)
            grad = jnp.where(core == 0, other, mine)
            normed, _ = normalize(pair.astype(F32))
            x = (normed * gain_ref[...] + shift_ref[...]).astype(BF16)
            wide = dot_nt(w_scr[0:256, :], x)
            q_t = wide[0:64].astype(BF16)
            gate = jax.nn.sigmoid(wide[64:128])
            k_t = wide[128:192].astype(BF16)
            v_t = wide[192:256].astype(BF16)
            dgated = dot_nt(w_scr[256:320, :], grad)
            dob_t = (dgated * gate).astype(BF16)
            kv = dot_nt(x, w_scr[128:256, :]).astype(BF16)
            row.update(x=x, grad=grad, gate=gate, dgated=dgated)
            for h in range(2):
                hs = slice(h * DH, (h + 1) * DH)
                slot = 4 * a + 2 * h
                rhs_scr[slot, hs, :] = q_t[hs]
                rhs_scr[slot + 1, 64 + h * DH : 64 + (h + 1) * DH, :] = dob_t[hs]
                items[h].update(a=a, h=h, slot=slot, kv=kv)
                items[h].update(q=q_t[hs], k=k_t[hs], v=v_t[hs], dob=dob_t[hs])

        def score(t):
            t["s"] = dot_nn(t["kv"], rhs_scr[t["slot"]]) * (scale * LOG2E) + bias_scr[t["h"]]

        def soften(t):
            expo = jnp.exp2(t["s"] - jnp.max(t["s"], axis=0, keepdims=True))
            t["p"] = expo * (1.0 / jnp.sum(expo, axis=0, keepdims=True))
            t["pb"] = t["p"].astype(BF16)

        def apply(t):
            t["o"] = dot_nn(t["v"], t["pb"])
            t["dp"] = dot_nn(t["kv"], rhs_scr[t["slot"] + 1])

        def back(t):
            delta = jnp.sum(t["dob"].astype(F32) * t["o"], axis=0, keepdims=True)
            ds = t["p"] * (t["dp"] - delta)
            t["dsb"] = ds.astype(BF16)
            t["dv"] = dot_nt(t["dob"], t["pb"])
            acc_scr[t["h"]] += ds

        def spread(t):
            h, here = t["h"], it * step_rows + t["a"]
            dq = dot_nn(t["k"], t["dsb"]) * scale
            dk = dot_nt(t["q"], t["dsb"]) * scale
            d_ref[here, h * DH : (h + 1) * DH, :] = dq.astype(BF16)
            d_ref[here, 128 + h * DH : 128 + (h + 1) * DH, :] = dk.astype(BF16)
            d_ref[here, 192 + h * DH : 192 + (h + 1) * DH, :] = t["dv"].astype(BF16)

        def finish(a, row, items):
            here = it * step_rows + a
            o_t = jnp.concatenate([items[0]["o"], items[1]["o"]], axis=0)
            gate = row["gate"]
            d_ref[here, 64:128, :] = (
                row["dgated"] * o_t * gate * (1.0 - gate)
            ).astype(BF16)
            wacc_scr[256:320, :] += dot_nn((gate * o_t).astype(BF16), row["grad"])
            pltpu.make_async_copy(d_ref.at[here], d_hbm.at[here], d_sems.at[here]).start()
            wacc_scr[0:256, :] += dot_nn(d_ref[here], row["x"])

        def forward(t):
            soften(t)
            apply(t)

        def backward(t):
            back(t)
            spread(t)

        stages = (score, forward, backward)
        depth = len(stages)
        plan = []
        for a in range(step_rows):
            row, items = {}, ({}, {})
            ready = lambda a=a, row=row, items=items: prepare(a, row, items)
            plan.append((2 * a - 1, 0, ready))
            for h in range(2):
                for place, stage in enumerate(stages):
                    when = 2 * a + h + place
                    plan.append((when, 1 + 2 * a + h, lambda stage=stage, t=items[h]: stage(t)))
            done = lambda a=a, row=row, items=items: finish(a, row, items)
            plan.append((2 * a + depth, 2 * a + 2.5, done))
        for _, _, act in sorted(plan, key=lambda e: (e[0], e[1])):
            act()
        return carry

    lax.fori_loop(0, groups // step_rows, some_rows, 0)

    for i in range(64):
        part = wacc_scr[5 * i : 5 * i + 8, :].astype(BF16)
        out_ref[2 * i, cols : cols + 8, :] = part
        out_ref[2 * i + 1, cols : cols + 8, :] = part
    copies = []
    for r in range(0, groups, 2):
        sl = slice(r * 64, r * 64 + 128)
        h0, h1 = acc_scr[0, :, sl], acc_scr[1, :, sl]
        b0 = jnp.where(low, h0, pltpu.roll(h1, 64, 1)).astype(BF16)
        b1 = jnp.where(low, pltpu.roll(h0, 64, 1), h1).astype(BF16)
        out_ref[r * blocks : (r + 1) * blocks, 0:cols, :] = b0.reshape(blocks, cols, C)
        out_ref[(r + 1) * blocks : (r + 2) * blocks, 0:cols, :] = b1.reshape(blocks, cols, C)
        part = pl.ds(r * blocks, 2 * blocks)
        copies.append(pltpu.make_async_copy(out_ref.at[part], out_hbm.at[part], sems.at[r // 2]))
        copies[-1].start()
    for r in range(groups):
        copies.append(pltpu.make_async_copy(d_ref.at[r], d_hbm.at[r], d_sems.at[r]))
    for copy in copies:
        copy.wait()


def dx_kernel(core_ref, mine_ref, other_ref, d_ref, w_ref, keep_ref, send_ref, norm_ref):
    core = core_ref[0]
    groups, blocks, cols = 8, 16, 32
    n, half = blocks * cols, cols // 2
    norm_ref[...] = jnp.zeros_like(norm_ref)

    def one_row(r, carry):
        src = pl.ds(r * blocks, blocks)
        mine = mine_ref[src, 0:cols, :].reshape(n, C)
        pair = jnp.where(core == 0, mine, other_ref[src, :, :].reshape(n, C))
        normed, _ = normalize(pair.astype(F32))
        dx = dot_tn(d_ref[r], w_ref[0:256, :])
        norm_ref[0:8, :] += jnp.sum((dx * normed).reshape(n // 8, 8, C), axis=0)
        norm_ref[8:16, :] += jnp.sum(dx.reshape(n // 8, 8, C), axis=0)
        dx = dx.astype(BF16).reshape(blocks, cols, C)
        keep_ref[src] = jnp.where(core == 0, dx[:, 0:half], dx[:, half:cols])
        send_ref[src] = jnp.where(core == 0, dx[:, half:cols], dx[:, 0:half])
        return carry

    lax.fori_loop(0, groups, one_row, 0, unroll=2)


def merge_kernel(keep_ref, came_ref, nt_ref, out_ref):
    devices, half = keep_ref.shape[0], keep_ref.shape[1]
    out_ref[:, 0:half, :] = nt_ref[...].reshape(devices, half, C)
    both = keep_ref[...].astype(F32) + came_ref[...].astype(F32)
    out_ref[:, half : 2 * half, :] = both.astype(BF16)


def sums_kernel(
    core_ref, held_ref, got_ref, norm_ref, gain_ref, shift_ref, wb_ref,
    z_ref, sums_hbm, z_scr, s_scr, sums_ref, sems,
):
    core = core_ref[0]
    rows, cols = got_ref.shape[0], 32
    last = pltpu.make_async_copy(held_ref.at[:, 16:32, :], sums_hbm.at[:, 16:32, :], sems.at[0])
    last.start()
    z_scr[...] = jnp.zeros_like(z_scr)
    for pair in range(2):

        def add(i, total, pair=pair):
            return total + got_ref[i, pair, 0:cols, :].astype(F32)

        total = lax.fori_loop(0, rows, add, jnp.zeros((cols, C), F32), unroll=8)
        for k in range(cols):
            for h in range(2):
                z_scr[2 * pair + h : 2 * pair + h + 1, k * rows : (k + 1) * rows] = total[
                    k : k + 1, h * 64 : (h + 1) * 64
                ]
    z = z_scr[...].astype(BF16)
    z_ref[...] = z
    nt = held_ref[:, 0:16, :].reshape(z.shape[1], C)
    dgn = dot_nn(z, nt)[0:4]
    total = jnp.sum(z_scr[0:4, :], axis=1, keepdims=True)

    def add_w(i, total):
        return total + got_ref[i, core, cols : cols + 8, :].astype(F32)

    s_scr[0:8, :] = lax.fori_loop(0, rows, add_w, jnp.zeros((8, C), F32), unroll=8)
    s_scr[8:12, :] = dgn * gain_ref[...] + total * shift_ref[...]
    wb = wb_ref[...].astype(F32)
    dgain = jnp.sum(norm_ref[0:8, :], axis=0, keepdims=True)
    dgain = dgain + jnp.sum(dgn * wb, axis=0, keepdims=True)
    dshift = jnp.sum(norm_ref[8:16, :], axis=0, keepdims=True)
    dshift = dshift + jnp.sum(total * wb, axis=0, keepdims=True)
    s_scr[12:13, :] = dgain
    s_scr[13:14, :] = dshift
    s_scr[14:15, :] = dgain - dgain.astype(BF16).astype(F32)
    s_scr[15:16, :] = dshift - dshift.astype(BF16).astype(F32)
    sums_ref[...] = jnp.broadcast_to(s_scr[...].astype(BF16)[None], sums_ref.shape)
    first = pltpu.make_async_copy(sums_ref, sums_hbm.at[:, 0:16, :], sems.at[1])
    first.start()
    last.wait()
    first.wait()


def ready_kernel(z_ref, pair_ref, gain_ref, wb_ref, ready_ref, dxb_scr, wb_scr):
    rows, cols = pair_ref.shape[0], pair_ref.shape[1]
    wb_scr[...] = jnp.zeros_like(wb_scr)
    wb_scr[0:4, :] = wb_ref[...].astype(F32)
    dxb_scr[...] = dot_tn(z_ref[...], wb_scr[...].astype(BF16))
    gain = gain_ref[...]

    def some(it, carry):
        i0 = it * 8
        part = pl.ds(i0, 8)
        normed, rstd = normalize(pair_ref[part].astype(F32))
        ready_ref[part, cols : 2 * cols, :] = normed.astype(BF16)
        ready_ref[part, 2 * cols : 3 * cols, :] = jnp.broadcast_to(rstd, normed.shape).astype(BF16)
        dxb = [dxb_scr[pl.ds(i0 + u, cols, stride=rows), :][None] for u in range(8)]
        dn = jnp.concatenate(dxb, axis=0) * gain
        base = rstd * (
            dn
            - jnp.mean(dn, axis=-1, keepdims=True)
            - normed * jnp.mean(dn * normed, axis=-1, keepdims=True)
        )
        ready_ref[part, 0:cols, :] = base.astype(BF16)
        return carry

    lax.fori_loop(0, rows // 8, some, 0)


def final_kernel(
    ready_ref, got_ref, gain_ref,
    dpair_hbm, dgain_ref, dshift_ref, dq_hbm, dk_hbm, dv_hbm, dg_hbm, db_ref, do_hbm,
    w_scr, dpair_ref, turn_scr, out_sems, w_sems,
):
    chips, cols, parts = got_ref.shape[0], dpair_ref.shape[1], out_sems.shape[0]
    size = chips // parts
    for core in range(2):
        for i in range(chips):
            w_scr[core, 5 * i : 5 * i + 8, :] = got_ref[i, core, 0:16, :].astype(F32)[0:8]
    sent = []
    for slot, out in enumerate((dq_hbm, dg_hbm, dk_hbm, dv_hbm)):
        sl = slice(slot * 64, (slot + 1) * 64)
        heads = jnp.concatenate([w_scr[0, sl, :], w_scr[1, sl, :]], axis=0)
        turn_scr[slot] = jnp.transpose(heads)
        sent.append(pltpu.make_async_copy(turn_scr.at[slot], out, w_sems.at[slot]))
    turn_scr[4, 0:64, :] = w_scr[0, 256:320, :]
    turn_scr[4, 64:128, :] = w_scr[1, 256:320, :]
    sent.append(pltpu.make_async_copy(turn_scr.at[4], do_hbm, w_sems.at[4]))
    for copy in sent:
        copy.start()
    zero = jnp.zeros((16, C), F32)

    def add(i, total):
        return total + (got_ref[i, 0, 0:16, :].astype(F32) + got_ref[i, 1, 0:16, :].astype(F32))

    total = lax.fori_loop(0, chips, add, zero, unroll=8)
    db_ref[...] = total[8:12]
    dgain_ref[...] = total[12:13] + total[14:15]
    dshift_ref[...] = total[13:14] + total[15:16]
    gain = gain_ref[...]
    for p in range(parts):
        part = pl.ds(p * size, size)
        normed = ready_ref[part, cols : 2 * cols, :].astype(F32).reshape(size * cols, C)
        dx = jnp.concatenate([got_ref[part, 0, 16:32, :], got_ref[part, 1, 16:32, :]], axis=1)
        dn = dx.astype(F32).reshape(size * cols, C) * gain
        out = dn - mean_lanes(dn) - normed * mean_lanes(dn * normed)
        rstd = ready_ref[part, 2 * cols : 3 * cols, :].astype(F32)
        out = out.reshape(size, cols, C) * rstd + ready_ref[part, 0:cols, :].astype(F32)
        dpair_ref[part] = out.astype(BF16)
        sent.append(pltpu.make_async_copy(dpair_ref.at[part], dpair_hbm.at[part], out_sems.at[p]))
        sent[-1].start()
    for copy in sent:
        copy.wait()


def on_device(
    pair, grad_out, norm_gain, norm_shift, w_query, w_key, w_value, w_gate, w_bias, w_out
):
    axes = ("row", "col")
    rows, cols = pair.shape[0], pair.shape[1]
    devices = 2 * rows
    sds = jax.ShapeDtypeStruct
    gain, shift = norm_gain.reshape(1, C), norm_shift.reshape(1, C)
    wb = w_bias.T
    core = (lax.axis_index("col") % 2).astype(jnp.int32).reshape(1)

    turned_scr = pltpu.VMEM((rows * cols, C), BF16)
    packed, nt = call(
        pack_kernel,
        (sds((rows, 2, 64, C), BF16), sds((rows * cols, C), BF16)),
        0,
        (
            pltpu.VMEM((rows * cols, C), F32),
            pltpu.VMEM((cols, C), F32),
            pltpu.VMEM((1, C), F32),
            pltpu.VMEM((1, C), F32),
            pltpu.VMEM((H, C), BF16),
            turned_scr,
            pltpu.SemaphoreType.DMA((5,)),
        ),
        hbm=5,
        flops=10**8,
        moved=4 * MIB,
    )(*(in_hbm(a) for a in (pair, grad_out, gain, shift, wb)))
    mine = lax.all_to_all(packed.reshape(devices, 64, C), axes, 0, 0, tiled=True)
    swap = [(i, i ^ 1) for i in range(16)]
    other = lax.ppermute(mine[:, 0:cols, :], "col", swap)
    terms, spread, turned_w = call(
        attend_kernel,
        (
            pltpu.HBM((devices, 40, C), BF16),
            pltpu.HBM((8, 256, 512), BF16),
            sds((320, C), BF16),
        ),
        9,
        (
            pltpu.VMEM((2, 512, 512), F32),
            pltpu.VMEM((2, 512, 512), F32),
            pltpu.VMEM((328, C), F32),
            pltpu.VMEM((16, C, 512), BF16),
            pltpu.VMEM((devices, 40, C), BF16),
            pltpu.VMEM((8, 256, 512), BF16),
            pltpu.SemaphoreType.DMA((4,)),
            pltpu.SemaphoreType.DMA((8,)),
        ),
        smem=1,
        to_hbm=(0, 1),
        vmem=36,
        flops=10**10,
        moved=6 * MIB,
    )(core, mine, other, gain, shift, w_query, w_key, w_value, w_gate, w_out)
    got = lax.all_to_all(terms, axes, 0, 0, tiled=True).reshape(rows, 2, 40, C)
    halves = sds((devices, cols // 2, C), BF16)
    keep, send, norms = call(
        dx_kernel,
        (halves, halves, sds((16, C), F32)),
        4,
        smem=1,
        flops=10**9,
        moved=6 * MIB,
    )(core, mine, other, spread, turned_w)
    came = lax.ppermute(send, "col", swap)
    held = call(
        merge_kernel, sds((devices, cols, C), BF16), 3, flops=10**7, moved=2 * MIB
    )(keep, came, nt)
    z, sums = call(
        sums_kernel,
        (sds((8, rows * cols), BF16), pltpu.HBM((devices, 32, C), BF16)),
        6,
        (
            pltpu.VMEM((8, rows * cols), F32),
            pltpu.VMEM((16, C), F32),
            pltpu.VMEM((devices, 16, C), BF16),
            pltpu.SemaphoreType.DMA((2,)),
        ),
        smem=1,
        to_hbm=(1,),
        flops=10**8,
        moved=4 * MIB,
    )(core, held, got, norms, gain, shift, wb)
    last = lax.all_to_all(sums, axes, 0, 0, tiled=True).reshape(rows, 2, 32, C)
    ready = call(
        ready_kernel,
        sds((rows, 3 * cols, C), BF16),
        4,
        (pltpu.VMEM((rows * cols, C), F32), pltpu.VMEM((8, C), F32)),
        flops=10**8,
        moved=8 * MIB,
    )(z, pair, gain, wb)
    square = pltpu.HBM((C, C), F32)
    d_pair, d_gain, d_shift, d_query, d_key, d_value, d_gate, d_bias, d_out = call(
        final_kernel,
        (
            pltpu.HBM(pair.shape, BF16),
            sds((1, C), F32),
            sds((1, C), F32),
            square,
            square,
            square,
            square,
            sds((H, C), F32),
            square,
        ),
        3,
        (
            pltpu.VMEM((2, 328, C), F32),
            pltpu.VMEM(pair.shape, BF16),
            pltpu.VMEM((5, C, C), F32),
            pltpu.SemaphoreType.DMA((4,)),
            pltpu.SemaphoreType.DMA((5,)),
        ),
        to_hbm=(0, 3, 4, 5, 6, 8),
        moved=8 * MIB,
    )(ready, last, gain)
    return (
        d_pair,
        d_gain.reshape(C),
        d_shift.reshape(C),
        d_query,
        d_key,
        d_value,
        d_gate,
        d_bias.T,
        d_out,
    )


def solution(mesh):
    return jax.shard_map(
        on_device,
        mesh=mesh,
        in_specs=(P("row", "col", None), P("row", "col", None)) + (P(),) * 8,
        out_specs=(P("row", "col", None),) + (P(),) * 8,
        check_vma=False,
    )
```

```python
import jax
import jax.numpy as jnp
from jax import lax
from jax.experimental import pallas as pl
from jax.experimental.pallas import tpu as pltpu
from jax.sharding import PartitionSpec as P

H = 4
DH = 32
C = 128
EPS = 1e-05
LOG2E = 1.4426950408889634
F32 = jnp.float32
BF16 = jnp.bfloat16
MIB = 1024 * 1024


def dot_nn(a, b):
    return lax.dot_general(a, b, (((1,), (0,)), ((), ())), preferred_element_type=F32)


def dot_nt(a, b):
    return lax.dot_general(a, b, (((1,), (1,)), ((), ())), preferred_element_type=F32)


def dot_tn(a, b):
    return lax.dot_general(a, b, (((0,), (0,)), ((), ())), preferred_element_type=F32)


def normalize(values):
    center = values - jnp.mean(values, axis=-1, keepdims=True)
    rstd = lax.rsqrt(jnp.mean(center * center, axis=-1, keepdims=True) + EPS)
    return center * rstd, rstd


def mean_lanes(values):
    return dot_nn(values.astype(BF16), jnp.full((C, C), 1.0 / C, BF16))


def call(
    kernel, out_shape, n_in, scratch=(), smem=0, hbm=0, to_hbm=(), vmem=16, flops=0, moved=0
):
    specs = [pl.BlockSpec(memory_space=pltpu.SMEM)] * smem
    specs += [pl.BlockSpec(memory_space=pltpu.HBM)] * hbm
    specs += [pl.BlockSpec(memory_space=pltpu.VMEM)] * n_in
    many = isinstance(out_shape, tuple)
    shapes = out_shape if many else (out_shape,)
    spaces = [pltpu.HBM if i in to_hbm else pltpu.VMEM for i in range(len(shapes))]
    outs = [pl.BlockSpec(memory_space=space) for space in spaces]
    outs = tuple(outs) if many else outs[0]
    return pl.pallas_call(
        kernel,
        out_shape=out_shape,
        in_specs=specs,
        out_specs=outs,
        scratch_shapes=list(scratch),
        cost_estimate=pl.CostEstimate(flops=flops, bytes_accessed=moved, transcendentals=0),
        compiler_params=pltpu.CompilerParams(vmem_limit_bytes=vmem * MIB),
    )


def in_hbm(array):
    return pltpu.with_memory_space_constraint(array, pltpu.HBM)


def pack_kernel(
    pair_hbm, grad_hbm, gain_hbm, shift_hbm, wb_hbm,
    out_ref, nt_ref, n_scr, b_scr, gain_scr, shift_scr, wb_scr, xt_ref, sems,
):
    rows, cols = pair_hbm.shape[0], pair_hbm.shape[1]
    copies = [
        pltpu.make_async_copy(src, dst, sems.at[i])
        for i, (src, dst) in enumerate(
            (
                (pair_hbm, out_ref.at[:, 0, 0:cols, :]),
                (gain_hbm, gain_scr),
                (shift_hbm, shift_scr),
                (wb_hbm, wb_scr),
                (grad_hbm, out_ref.at[:, 1, 0:cols, :]),
            )
        )
    ]
    for copy in copies:
        copy.start()
    for copy in copies[:-1]:
        copy.wait()
    normed, _ = normalize(out_ref[:, 0, 0:cols, :].reshape(rows * cols, C).astype(F32))
    n_scr[...] = normed
    for k in range(cols):
        part = n_scr[pl.ds(k, rows, stride=cols), :]
        nt_ref[k * rows : (k + 1) * rows, :] = part.astype(BF16)
        xt_ref[k * rows : (k + 1) * rows, :] = (part * gain_scr[...] + shift_scr[...]).astype(BF16)
    bias = dot_nt(wb_scr[...], xt_ref[...])
    for pair in range(2):
        for k in range(cols):
            part = bias[2 * pair : 2 * pair + 2, k * rows : (k + 1) * rows]
            b_scr[k : k + 1, :] = jnp.concatenate([part[0:1], part[1:2]], axis=1)
        packed = b_scr[...].astype(BF16)
        out_ref[:, pair, cols : 2 * cols, :] = jnp.broadcast_to(packed[None], (rows, cols, C))
    copies[-1].wait()


def prepare_kernel(core_ref, mine_ref, wq_ref, wk_ref, wv_ref, wg_ref, wo_ref, bias_ref, w_ref):
    core = core_ref[0]
    groups, blocks, cols = 8, 16, 32
    n = blocks * cols
    low = lax.broadcasted_iota(jnp.int32, (n, C), 1) < 64
    for slot, ref in enumerate((wq_ref, wg_ref, wk_ref, wv_ref)):
        turned = jnp.transpose(ref[...].astype(F32)).astype(BF16)
        w_ref[slot * 64 : (slot + 1) * 64, :] = jnp.where(core == 0, turned[0:64], turned[64:128])
    w_ref[256:320, :] = jnp.where(core == 0, wo_ref[0:64, :], wo_ref[64:128, :])
    for r in range(0, groups, 2):
        b0 = mine_ref[r * blocks : (r + 1) * blocks, cols : 2 * cols, :].reshape(n, C).astype(F32)
        b1 = mine_ref[(r + 1) * blocks : (r + 2) * blocks, cols : 2 * cols, :].reshape(n, C)
        b1 = b1.astype(F32)
        sl = slice(r * 64, r * 64 + 128)
        bias_ref[0, :, sl] = jnp.where(low, b0, pltpu.roll(b1, 64, 1)) * LOG2E
        bias_ref[1, :, sl] = jnp.where(low, pltpu.roll(b0, 64, 1), b1) * LOG2E


def attend_kernel(
    core_ref, mine_ref, other_ref, gain_ref, shift_ref, bias_ref, w_ref,
    out_hbm, d_hbm, acc_scr, wacc_scr, rhs_scr, out_ref, d_ref, sems, d_sems,
):
    core = core_ref[0]
    groups, blocks, cols, step_rows = 8, 16, 32, 4
    n = blocks * cols
    scale = DH ** (-0.5)
    lane = lax.broadcasted_iota(jnp.int32, (n, C), 1)
    low = lane < 64
    acc_scr[...] = jnp.zeros_like(acc_scr)
    wacc_scr[...] = jnp.zeros_like(wacc_scr)
    rhs_scr[...] = jnp.zeros_like(rhs_scr)

    def some_rows(it, carry):
        def prepare(a, row, items):
            src = pl.ds((it * step_rows + a) * blocks, blocks)
            mine = mine_ref[src, 0:cols, :].reshape(n, C)
            other = other_ref[src, :, :].reshape(n, C)
            pair = jnp.where(core == 0, mine, other)
            grad = jnp.where(core == 0, other, mine)
            normed, _ = normalize(pair.astype(F32))
            x = (normed * gain_ref[...] + shift_ref[...]).astype(BF16)
            wide = dot_nt(w_ref[0:256, :], x)
            q_t = wide[0:64].astype(BF16)
            gate = jax.nn.sigmoid(wide[64:128])
            k_t = wide[128:192].astype(BF16)
            v_t = wide[192:256].astype(BF16)
            dgated = dot_nt(w_ref[256:320, :], grad)
            dob_t = (dgated * gate).astype(BF16)
            kv = dot_nt(x, w_ref[128:256, :]).astype(BF16)
            row.update(x=x, grad=grad, gate=gate, dgated=dgated)
            for h in range(2):
                hs = slice(h * DH, (h + 1) * DH)
                slot = 4 * a + 2 * h
                rhs_scr[slot, hs, :] = q_t[hs]
                rhs_scr[slot + 1, 64 + h * DH : 64 + (h + 1) * DH, :] = dob_t[hs]
                items[h].update(a=a, h=h, slot=slot, kv=kv)
                items[h].update(q=q_t[hs], k=k_t[hs], v=v_t[hs], dob=dob_t[hs])

        def score(t):
            t["s"] = dot_nn(t["kv"], rhs_scr[t["slot"]]) * (scale * LOG2E) + bias_ref[t["h"]]

        def soften(t):
            expo = jnp.exp2(t["s"] - jnp.max(t["s"], axis=0, keepdims=True))
            t["p"] = expo * (1.0 / jnp.sum(expo, axis=0, keepdims=True))
            t["pb"] = t["p"].astype(BF16)

        def apply(t):
            t["o"] = dot_nn(t["v"], t["pb"])
            t["dp"] = dot_nn(t["kv"], rhs_scr[t["slot"] + 1])

        def back(t):
            delta = jnp.sum(t["dob"].astype(F32) * t["o"], axis=0, keepdims=True)
            ds = t["p"] * (t["dp"] - delta)
            t["dsb"] = ds.astype(BF16)
            t["dv"] = dot_nt(t["dob"], t["pb"])
            acc_scr[t["h"]] += ds

        def spread(t):
            h, here = t["h"], it * step_rows + t["a"]
            dq = dot_nn(t["k"], t["dsb"]) * scale
            dk = dot_nt(t["q"], t["dsb"]) * scale
            d_ref[here, h * DH : (h + 1) * DH, :] = dq.astype(BF16)
            d_ref[here, 128 + h * DH : 128 + (h + 1) * DH, :] = dk.astype(BF16)
            d_ref[here, 192 + h * DH : 192 + (h + 1) * DH, :] = t["dv"].astype(BF16)

        def finish(a, row, items):
            here = it * step_rows + a
            o_t = jnp.concatenate([items[0]["o"], items[1]["o"]], axis=0)
            gate = row["gate"]
            d_ref[here, 64:128, :] = (
                row["dgated"] * o_t * gate * (1.0 - gate)
            ).astype(BF16)
            wacc_scr[256:320, :] += dot_nn((gate * o_t).astype(BF16), row["grad"])
            pltpu.make_async_copy(d_ref.at[here], d_hbm.at[here], d_sems.at[here]).start()
            wacc_scr[0:256, :] += dot_nn(d_ref[here], row["x"])

        def forward(t):
            soften(t)
            apply(t)

        def backward(t):
            back(t)
            spread(t)

        stages = (score, forward, backward)
        depth = len(stages)
        plan = []
        for a in range(step_rows):
            row, items = {}, ({}, {})
            ready = lambda a=a, row=row, items=items: prepare(a, row, items)
            plan.append((2 * a - 1, 0, ready))
            for h in range(2):
                for place, stage in enumerate(stages):
                    when = 2 * a + h + place
                    plan.append((when, 1 + 2 * a + h, lambda stage=stage, t=items[h]: stage(t)))
            done = lambda a=a, row=row, items=items: finish(a, row, items)
            plan.append((2 * a + depth, 2 * a + 2.5, done))
        for _, _, act in sorted(plan, key=lambda e: (e[0], e[1])):
            act()
        return carry

    lax.fori_loop(0, groups // step_rows, some_rows, 0)

    for i in range(64):
        part = wacc_scr[5 * i : 5 * i + 8, :].astype(BF16)
        out_ref[2 * i, cols : cols + 8, :] = part
        out_ref[2 * i + 1, cols : cols + 8, :] = part
    copies = []
    for r in range(0, groups, 2):
        sl = slice(r * 64, r * 64 + 128)
        h0, h1 = acc_scr[0, :, sl], acc_scr[1, :, sl]
        b0 = jnp.where(low, h0, pltpu.roll(h1, 64, 1)).astype(BF16)
        b1 = jnp.where(low, pltpu.roll(h0, 64, 1), h1).astype(BF16)
        out_ref[r * blocks : (r + 1) * blocks, 0:cols, :] = b0.reshape(blocks, cols, C)
        out_ref[(r + 1) * blocks : (r + 2) * blocks, 0:cols, :] = b1.reshape(blocks, cols, C)
        part = pl.ds(r * blocks, 2 * blocks)
        copies.append(pltpu.make_async_copy(out_ref.at[part], out_hbm.at[part], sems.at[r // 2]))
        copies[-1].start()
    for r in range(groups):
        copies.append(pltpu.make_async_copy(d_ref.at[r], d_hbm.at[r], d_sems.at[r]))
    for copy in copies:
        copy.wait()


def dx_kernel(core_ref, mine_ref, other_ref, d_ref, w_ref, keep_ref, send_ref, norm_ref):
    core = core_ref[0]
    groups, blocks, cols = 8, 16, 32
    n, half = blocks * cols, cols // 2
    norm_ref[...] = jnp.zeros_like(norm_ref)

    def one_row(r, carry):
        src = pl.ds(r * blocks, blocks)
        mine = mine_ref[src, 0:cols, :].reshape(n, C)
        pair = jnp.where(core == 0, mine, other_ref[src, :, :].reshape(n, C))
        normed, _ = normalize(pair.astype(F32))
        dx = dot_tn(d_ref[r], w_ref[0:256, :])
        norm_ref[0:8, :] += jnp.sum((dx * normed).reshape(n // 8, 8, C), axis=0)
        norm_ref[8:16, :] += jnp.sum(dx.reshape(n // 8, 8, C), axis=0)
        dx = dx.astype(BF16).reshape(blocks, cols, C)
        keep_ref[src] = jnp.where(core == 0, dx[:, 0:half], dx[:, half:cols])
        send_ref[src] = jnp.where(core == 0, dx[:, half:cols], dx[:, 0:half])
        return carry

    lax.fori_loop(0, groups, one_row, 0, unroll=2)


def merge_kernel(keep_ref, came_ref, nt_ref, out_ref):
    devices, half = keep_ref.shape[0], keep_ref.shape[1]
    out_ref[:, 0:half, :] = nt_ref[...].reshape(devices, half, C)
    both = keep_ref[...].astype(F32) + came_ref[...].astype(F32)
    out_ref[:, half : 2 * half, :] = both.astype(BF16)


def sums_kernel(
    core_ref, held_ref, got_ref, norm_ref, gain_ref, shift_ref, wb_ref,
    z_ref, sums_hbm, z_scr, s_scr, sums_ref, sems,
):
    core = core_ref[0]
    rows, cols = got_ref.shape[0], 32
    last = pltpu.make_async_copy(held_ref.at[:, 16:32, :], sums_hbm.at[:, 16:32, :], sems.at[0])
    last.start()
    z_scr[...] = jnp.zeros_like(z_scr)
    for pair in range(2):

        def add(i, total, pair=pair):
            return total + got_ref[i, pair, 0:cols, :].astype(F32)

        total = lax.fori_loop(0, rows, add, jnp.zeros((cols, C), F32), unroll=8)
        for k in range(cols):
            for h in range(2):
                z_scr[2 * pair + h : 2 * pair + h + 1, k * rows : (k + 1) * rows] = total[
                    k : k + 1, h * 64 : (h + 1) * 64
                ]
    z = z_scr[...].astype(BF16)
    z_ref[...] = z
    nt = held_ref[:, 0:16, :].reshape(z.shape[1], C)
    dgn = dot_nn(z, nt)[0:4]
    total = jnp.sum(z_scr[0:4, :], axis=1, keepdims=True)

    def add_w(i, total):
        return total + got_ref[i, core, cols : cols + 8, :].astype(F32)

    s_scr[0:8, :] = lax.fori_loop(0, rows, add_w, jnp.zeros((8, C), F32), unroll=8)
    s_scr[8:12, :] = dgn * gain_ref[...] + total * shift_ref[...]
    wb = wb_ref[...].astype(F32)
    dgain = jnp.sum(norm_ref[0:8, :], axis=0, keepdims=True)
    dgain = dgain + jnp.sum(dgn * wb, axis=0, keepdims=True)
    dshift = jnp.sum(norm_ref[8:16, :], axis=0, keepdims=True)
    dshift = dshift + jnp.sum(total * wb, axis=0, keepdims=True)
    s_scr[12:13, :] = dgain
    s_scr[13:14, :] = dshift
    s_scr[14:15, :] = dgain - dgain.astype(BF16).astype(F32)
    s_scr[15:16, :] = dshift - dshift.astype(BF16).astype(F32)
    sums_ref[...] = jnp.broadcast_to(s_scr[...].astype(BF16)[None], sums_ref.shape)
    first = pltpu.make_async_copy(sums_ref, sums_hbm.at[:, 0:16, :], sems.at[1])
    first.start()
    last.wait()
    first.wait()


def ready_kernel(z_ref, pair_ref, gain_ref, wb_ref, ready_ref, dxb_scr, wb_scr):
    rows, cols = pair_ref.shape[0], pair_ref.shape[1]
    wb_scr[...] = jnp.zeros_like(wb_scr)
    wb_scr[0:4, :] = wb_ref[...].astype(F32)
    dxb_scr[...] = dot_tn(z_ref[...], wb_scr[...].astype(BF16))
    gain = gain_ref[...]

    def some(it, carry):
        i0 = it * 8
        part = pl.ds(i0, 8)
        normed, rstd = normalize(pair_ref[part].astype(F32))
        ready_ref[part, cols : 2 * cols, :] = normed.astype(BF16)
        ready_ref[part, 2 * cols : 3 * cols, :] = jnp.broadcast_to(rstd, normed.shape).astype(BF16)
        dxb = [dxb_scr[pl.ds(i0 + u, cols, stride=rows), :][None] for u in range(8)]
        dn = jnp.concatenate(dxb, axis=0) * gain
        base = rstd * (
            dn
            - jnp.mean(dn, axis=-1, keepdims=True)
            - normed * jnp.mean(dn * normed, axis=-1, keepdims=True)
        )
        ready_ref[part, 0:cols, :] = base.astype(BF16)
        return carry

    lax.fori_loop(0, rows // 8, some, 0)


def final_kernel(
    ready_ref, got_ref, gain_ref,
    dpair_hbm, dgain_ref, dshift_ref, dq_hbm, dk_hbm, dv_hbm, dg_hbm, db_ref, do_hbm,
    w_scr, dpair_ref, turn_scr, out_sems, w_sems,
):
    chips, cols, parts = got_ref.shape[0], dpair_ref.shape[1], out_sems.shape[0]
    size = chips // parts
    for core in range(2):
        for i in range(chips):
            w_scr[core, 5 * i : 5 * i + 8, :] = got_ref[i, core, 0:16, :].astype(F32)[0:8]
    sent = []
    for slot, out in enumerate((dq_hbm, dg_hbm, dk_hbm, dv_hbm)):
        sl = slice(slot * 64, (slot + 1) * 64)
        heads = jnp.concatenate([w_scr[0, sl, :], w_scr[1, sl, :]], axis=0)
        turn_scr[slot] = jnp.transpose(heads)
        sent.append(pltpu.make_async_copy(turn_scr.at[slot], out, w_sems.at[slot]))
    turn_scr[4, 0:64, :] = w_scr[0, 256:320, :]
    turn_scr[4, 64:128, :] = w_scr[1, 256:320, :]
    sent.append(pltpu.make_async_copy(turn_scr.at[4], do_hbm, w_sems.at[4]))
    for copy in sent:
        copy.start()
    zero = jnp.zeros((16, C), F32)

    def add(i, total):
        return total + (got_ref[i, 0, 0:16, :].astype(F32) + got_ref[i, 1, 0:16, :].astype(F32))

    total = lax.fori_loop(0, chips, add, zero, unroll=8)
    db_ref[...] = total[8:12]
    dgain_ref[...] = total[12:13] + total[14:15]
    dshift_ref[...] = total[13:14] + total[15:16]
    gain = gain_ref[...]
    for p in range(parts):
        part = pl.ds(p * size, size)
        normed = ready_ref[part, cols : 2 * cols, :].astype(F32).reshape(size * cols, C)
        dx = jnp.concatenate([got_ref[part, 0, 16:32, :], got_ref[part, 1, 16:32, :]], axis=1)
        dn = dx.astype(F32).reshape(size * cols, C) * gain
        out = dn - mean_lanes(dn) - normed * mean_lanes(dn * normed)
        rstd = ready_ref[part, 2 * cols : 3 * cols, :].astype(F32)
        out = out.reshape(size, cols, C) * rstd + ready_ref[part, 0:cols, :].astype(F32)
        dpair_ref[part] = out.astype(BF16)
        sent.append(pltpu.make_async_copy(dpair_ref.at[part], dpair_hbm.at[part], out_sems.at[p]))
        sent[-1].start()
    for copy in sent:
        copy.wait()


def on_device(
    pair, grad_out, norm_gain, norm_shift, w_query, w_key, w_value, w_gate, w_bias, w_out
):
    axes = ("row", "col")
    rows, cols = pair.shape[0], pair.shape[1]
    devices = 2 * rows
    sds = jax.ShapeDtypeStruct
    gain, shift = norm_gain.reshape(1, C), norm_shift.reshape(1, C)
    wb = w_bias.T
    core = (lax.axis_index("col") % 2).astype(jnp.int32).reshape(1)

    turned_scr = pltpu.VMEM((rows * cols, C), BF16)
    packed, nt = call(
        pack_kernel,
        (sds((rows, 2, 64, C), BF16), sds((rows * cols, C), BF16)),
        0,
        (
            pltpu.VMEM((rows * cols, C), F32),
            pltpu.VMEM((cols, C), F32),
            pltpu.VMEM((1, C), F32),
            pltpu.VMEM((1, C), F32),
            pltpu.VMEM((H, C), BF16),
            turned_scr,
            pltpu.SemaphoreType.DMA((5,)),
        ),
        hbm=5,
        flops=10**8,
        moved=4 * MIB,
    )(*(in_hbm(a) for a in (pair, grad_out, gain, shift, wb)))
    mine = lax.all_to_all(packed.reshape(devices, 64, C), axes, 0, 0, tiled=True)
    swap = [(i, i ^ 1) for i in range(16)]
    other = lax.ppermute(mine[:, 0:cols, :], "col", swap)
    bias, turned_w = call(
        prepare_kernel,
        (sds((2, 512, 512), F32), sds((320, C), BF16)),
        6,
        smem=1,
        flops=10**8,
        moved=4 * MIB,
    )(core, mine, w_query, w_key, w_value, w_gate, w_out)
    terms, spread = call(
        attend_kernel,
        (pltpu.HBM((devices, 40, C), BF16), pltpu.HBM((8, 256, 512), BF16)),
        6,
        (
            pltpu.VMEM((2, 512, 512), F32),
            pltpu.VMEM((328, C), F32),
            pltpu.VMEM((16, C, 512), BF16),
            pltpu.VMEM((devices, 40, C), BF16),
            pltpu.VMEM((8, 256, 512), BF16),
            pltpu.SemaphoreType.DMA((4,)),
            pltpu.SemaphoreType.DMA((8,)),
        ),
        smem=1,
        to_hbm=(0, 1),
        vmem=24,
        flops=10**10,
        moved=6 * MIB,
    )(core, mine, other, gain, shift, bias, turned_w)
    got = lax.all_to_all(terms, axes, 0, 0, tiled=True).reshape(rows, 2, 40, C)
    halves = sds((devices, cols // 2, C), BF16)
    keep, send, norms = call(
        dx_kernel,
        (halves, halves, sds((16, C), F32)),
        4,
        smem=1,
        flops=10**9,
        moved=6 * MIB,
    )(core, mine, other, spread, turned_w)
    came = lax.ppermute(send, "col", swap)
    held = call(
        merge_kernel, sds((devices, cols, C), BF16), 3, flops=10**7, moved=2 * MIB
    )(keep, came, nt)
    z, sums = call(
        sums_kernel,
        (sds((8, rows * cols), BF16), pltpu.HBM((devices, 32, C), BF16)),
        6,
        (
            pltpu.VMEM((8, rows * cols), F32),
            pltpu.VMEM((16, C), F32),
            pltpu.VMEM((devices, 16, C), BF16),
            pltpu.SemaphoreType.DMA((2,)),
        ),
        smem=1,
        to_hbm=(1,),
        flops=10**8,
        moved=4 * MIB,
    )(core, held, got, norms, gain, shift, wb)
    last = lax.all_to_all(sums, axes, 0, 0, tiled=True).reshape(rows, 2, 32, C)
    ready = call(
        ready_kernel,
        sds((rows, 3 * cols, C), BF16),
        4,
        (pltpu.VMEM((rows * cols, C), F32), pltpu.VMEM((8, C), F32)),
        flops=10**8,
        moved=8 * MIB,
    )(z, pair, gain, wb)
    square = pltpu.HBM((C, C), F32)
    d_pair, d_gain, d_shift, d_query, d_key, d_value, d_gate, d_bias, d_out = call(
        final_kernel,
        (
            pltpu.HBM(pair.shape, BF16),
            sds((1, C), F32),
            sds((1, C), F32),
            square,
            square,
            square,
            square,
            sds((H, C), F32),
            square,
        ),
        3,
        (
            pltpu.VMEM((2, 328, C), F32),
            pltpu.VMEM(pair.shape, BF16),
            pltpu.VMEM((5, C, C), F32),
            pltpu.SemaphoreType.DMA((4,)),
            pltpu.SemaphoreType.DMA((5,)),
        ),
        to_hbm=(0, 3, 4, 5, 6, 8),
        moved=8 * MIB,
    )(ready, last, gain)
    return (
        d_pair,
        d_gain.reshape(C),
        d_shift.reshape(C),
        d_query,
        d_key,
        d_value,
        d_gate,
        d_bias.T,
        d_out,
    )


def solution(mesh):
    return jax.shard_map(
        on_device,
        mesh=mesh,
        in_specs=(P("row", "col", None), P("row", "col", None)) + (P(),) * 8,
        out_specs=(P("row", "col", None),) + (P(),) * 8,
        check_vma=False,
    )
```

```python
import jax
import jax.numpy as jnp
from jax import lax
from jax.experimental import pallas as pl
from jax.experimental.pallas import tpu as pltpu
from jax.sharding import PartitionSpec as P

H = 4
DH = 32
C = 128
EPS = 1e-05
LOG2E = 1.4426950408889634
F32 = jnp.float32
BF16 = jnp.bfloat16
MIB = 1024 * 1024


def dot_nn(a, b):
    return lax.dot_general(a, b, (((1,), (0,)), ((), ())), preferred_element_type=F32)


def dot_nt(a, b):
    return lax.dot_general(a, b, (((1,), (1,)), ((), ())), preferred_element_type=F32)


def dot_tn(a, b):
    return lax.dot_general(a, b, (((0,), (0,)), ((), ())), preferred_element_type=F32)


def normalize(values):
    center = values - jnp.mean(values, axis=-1, keepdims=True)
    rstd = lax.rsqrt(jnp.mean(center * center, axis=-1, keepdims=True) + EPS)
    return center * rstd, rstd


def mean_lanes(values):
    return dot_nn(values.astype(BF16), jnp.full((C, C), 1.0 / C, BF16))


def call(
    kernel, out_shape, n_in, scratch=(), smem=0, hbm=0, to_hbm=(), vmem=16, flops=0, moved=0
):
    specs = [pl.BlockSpec(memory_space=pltpu.SMEM)] * smem
    specs += [pl.BlockSpec(memory_space=pltpu.HBM)] * hbm
    specs += [pl.BlockSpec(memory_space=pltpu.VMEM)] * n_in
    many = isinstance(out_shape, tuple)
    shapes = out_shape if many else (out_shape,)
    spaces = [pltpu.HBM if i in to_hbm else pltpu.VMEM for i in range(len(shapes))]
    outs = [pl.BlockSpec(memory_space=space) for space in spaces]
    outs = tuple(outs) if many else outs[0]
    return pl.pallas_call(
        kernel,
        out_shape=out_shape,
        in_specs=specs,
        out_specs=outs,
        scratch_shapes=list(scratch),
        cost_estimate=pl.CostEstimate(flops=flops, bytes_accessed=moved, transcendentals=0),
        compiler_params=pltpu.CompilerParams(vmem_limit_bytes=vmem * MIB),
    )


def in_hbm(array):
    return pltpu.with_memory_space_constraint(array, pltpu.HBM)


def pack_kernel(
    pair_hbm, grad_hbm, gain_hbm, shift_hbm, wb_hbm,
    out_ref, nt_ref, n_scr, b_scr, gain_scr, shift_scr, wb_scr, xt_ref, sems,
):
    rows, cols = pair_hbm.shape[0], pair_hbm.shape[1]
    copies = [
        pltpu.make_async_copy(src, dst, sems.at[i])
        for i, (src, dst) in enumerate(
            (
                (pair_hbm.at[0 : rows // 2], out_ref.at[0 : rows // 2, 0, 0:cols, :]),
                (pair_hbm.at[rows // 2 : rows], out_ref.at[rows // 2 : rows, 0, 0:cols, :]),
                (gain_hbm, gain_scr),
                (shift_hbm, shift_scr),
                (wb_hbm, wb_scr),
                (grad_hbm, out_ref.at[:, 1, 0:cols, :]),
            )
        )
    ]
    for copy in copies:
        copy.start()
    size = rows * cols // 2
    for p in range(2):
        copies[p].wait()
        part = out_ref[p * rows // 2 : (p + 1) * rows // 2, 0, 0:cols, :]
        n_scr[p * size : (p + 1) * size, :] = normalize(part.reshape(size, C).astype(F32))[0]
    for copy in copies[2:-1]:
        copy.wait()
    for k in range(cols):
        part = n_scr[pl.ds(k, rows, stride=cols), :]
        nt_ref[k * rows : (k + 1) * rows, :] = part.astype(BF16)
        xt_ref[k * rows : (k + 1) * rows, :] = (part * gain_scr[...] + shift_scr[...]).astype(BF16)
    bias = dot_nt(wb_scr[...], xt_ref[...])
    for pair in range(2):
        for k in range(cols):
            part = bias[2 * pair : 2 * pair + 2, k * rows : (k + 1) * rows]
            b_scr[k : k + 1, :] = jnp.concatenate([part[0:1], part[1:2]], axis=1)
        packed = b_scr[...].astype(BF16)
        out_ref[:, pair, cols : 2 * cols, :] = jnp.broadcast_to(packed[None], (rows, cols, C))
    copies[-1].wait()


def prepare_kernel(core_ref, mine_ref, wq_ref, wk_ref, wv_ref, wg_ref, wo_ref, bias_ref, w_ref):
    core = core_ref[0]
    groups, blocks, cols = 8, 16, 32
    n = blocks * cols
    low = lax.broadcasted_iota(jnp.int32, (n, C), 1) < 64
    for slot, ref in enumerate((wq_ref, wg_ref, wk_ref, wv_ref)):
        turned = jnp.transpose(ref[...].astype(F32)).astype(BF16)
        w_ref[slot * 64 : (slot + 1) * 64, :] = jnp.where(core == 0, turned[0:64], turned[64:128])
    w_ref[256:320, :] = jnp.where(core == 0, wo_ref[0:64, :], wo_ref[64:128, :])
    for r in range(0, groups, 2):
        b0 = mine_ref[r * blocks : (r + 1) * blocks, cols : 2 * cols, :].reshape(n, C).astype(F32)
        b1 = mine_ref[(r + 1) * blocks : (r + 2) * blocks, cols : 2 * cols, :].reshape(n, C)
        b1 = b1.astype(F32)
        sl = slice(r * 64, r * 64 + 128)
        bias_ref[0, :, sl] = jnp.where(low, b0, pltpu.roll(b1, 64, 1)) * LOG2E
        bias_ref[1, :, sl] = jnp.where(low, pltpu.roll(b0, 64, 1), b1) * LOG2E


def attend_kernel(
    core_ref, mine_ref, other_ref, gain_ref, shift_ref, bias_ref, w_ref,
    out_hbm, d_hbm, acc_scr, wacc_scr, rhs_scr, out_ref, d_ref, sems, d_sems,
):
    core = core_ref[0]
    groups, blocks, cols, step_rows = 8, 16, 32, 4
    n = blocks * cols
    scale = DH ** (-0.5)
    lane = lax.broadcasted_iota(jnp.int32, (n, C), 1)
    low = lane < 64
    acc_scr[...] = jnp.zeros_like(acc_scr)
    wacc_scr[...] = jnp.zeros_like(wacc_scr)
    rhs_scr[...] = jnp.zeros_like(rhs_scr)

    def some_rows(it, carry):
        def prepare(a, row, items):
            src = pl.ds((it * step_rows + a) * blocks, blocks)
            mine = mine_ref[src, 0:cols, :].reshape(n, C)
            other = other_ref[src, :, :].reshape(n, C)
            pair = jnp.where(core == 0, mine, other)
            grad = jnp.where(core == 0, other, mine)
            normed, _ = normalize(pair.astype(F32))
            x = (normed * gain_ref[...] + shift_ref[...]).astype(BF16)
            wide = dot_nt(w_ref[0:256, :], x)
            q_t = wide[0:64].astype(BF16)
            gate = jax.nn.sigmoid(wide[64:128])
            k_t = wide[128:192].astype(BF16)
            v_t = wide[192:256].astype(BF16)
            dgated = dot_nt(w_ref[256:320, :], grad)
            dob_t = (dgated * gate).astype(BF16)
            kv = dot_nt(x, w_ref[128:256, :]).astype(BF16)
            row.update(x=x, grad=grad, gate=gate, dgated=dgated)
            for h in range(2):
                hs = slice(h * DH, (h + 1) * DH)
                slot = 4 * a + 2 * h
                rhs_scr[slot, hs, :] = q_t[hs]
                rhs_scr[slot + 1, 64 + h * DH : 64 + (h + 1) * DH, :] = dob_t[hs]
                items[h].update(a=a, h=h, slot=slot, kv=kv)
                items[h].update(q=q_t[hs], k=k_t[hs], v=v_t[hs], dob=dob_t[hs])

        def score(t):
            t["s"] = dot_nn(t["kv"], rhs_scr[t["slot"]]) * (scale * LOG2E) + bias_ref[t["h"]]

        def soften(t):
            expo = jnp.exp2(t["s"] - jnp.max(t["s"], axis=0, keepdims=True))
            t["p"] = expo * (1.0 / jnp.sum(expo, axis=0, keepdims=True))
            t["pb"] = t["p"].astype(BF16)

        def apply(t):
            t["o"] = dot_nn(t["v"], t["pb"])
            t["dp"] = dot_nn(t["kv"], rhs_scr[t["slot"] + 1])

        def back(t):
            delta = jnp.sum(t["dob"].astype(F32) * t["o"], axis=0, keepdims=True)
            ds = t["p"] * (t["dp"] - delta)
            t["dsb"] = ds.astype(BF16)
            t["dv"] = dot_nt(t["dob"], t["pb"])
            acc_scr[t["h"]] += ds

        def spread(t):
            h, here = t["h"], it * step_rows + t["a"]
            dq = dot_nn(t["k"], t["dsb"]) * scale
            dk = dot_nt(t["q"], t["dsb"]) * scale
            d_ref[here, h * DH : (h + 1) * DH, :] = dq.astype(BF16)
            d_ref[here, 128 + h * DH : 128 + (h + 1) * DH, :] = dk.astype(BF16)
            d_ref[here, 192 + h * DH : 192 + (h + 1) * DH, :] = t["dv"].astype(BF16)

        def finish(a, row, items):
            here = it * step_rows + a
            o_t = jnp.concatenate([items[0]["o"], items[1]["o"]], axis=0)
            gate = row["gate"]
            d_ref[here, 64:128, :] = (
                row["dgated"] * o_t * gate * (1.0 - gate)
            ).astype(BF16)
            wacc_scr[256:320, :] += dot_nn((gate * o_t).astype(BF16), row["grad"])
            pltpu.make_async_copy(d_ref.at[here], d_hbm.at[here], d_sems.at[here]).start()
            wacc_scr[0:256, :] += dot_nn(d_ref[here], row["x"])

        def forward(t):
            soften(t)
            apply(t)

        def backward(t):
            back(t)
            spread(t)

        stages = (score, forward, backward)
        depth = len(stages)
        plan = []
        for a in range(step_rows):
            row, items = {}, ({}, {})
            ready = lambda a=a, row=row, items=items: prepare(a, row, items)
            plan.append((2 * a - 1, 0, ready))
            for h in range(2):
                for place, stage in enumerate(stages):
                    when = 2 * a + h + place
                    plan.append((when, 1 + 2 * a + h, lambda stage=stage, t=items[h]: stage(t)))
            done = lambda a=a, row=row, items=items: finish(a, row, items)
            plan.append((2 * a + depth, 2 * a + 2.5, done))
        for _, _, act in sorted(plan, key=lambda e: (e[0], e[1])):
            act()
        return carry

    lax.fori_loop(0, groups // step_rows, some_rows, 0)

    for i in range(64):
        part = wacc_scr[5 * i : 5 * i + 8, :].astype(BF16)
        out_ref[2 * i, cols : cols + 8, :] = part
        out_ref[2 * i + 1, cols : cols + 8, :] = part
    copies = []
    for r in range(0, groups, 2):
        sl = slice(r * 64, r * 64 + 128)
        h0, h1 = acc_scr[0, :, sl], acc_scr[1, :, sl]
        b0 = jnp.where(low, h0, pltpu.roll(h1, 64, 1)).astype(BF16)
        b1 = jnp.where(low, pltpu.roll(h0, 64, 1), h1).astype(BF16)
        out_ref[r * blocks : (r + 1) * blocks, 0:cols, :] = b0.reshape(blocks, cols, C)
        out_ref[(r + 1) * blocks : (r + 2) * blocks, 0:cols, :] = b1.reshape(blocks, cols, C)
        part = pl.ds(r * blocks, 2 * blocks)
        copies.append(pltpu.make_async_copy(out_ref.at[part], out_hbm.at[part], sems.at[r // 2]))
        copies[-1].start()
    for r in range(groups):
        copies.append(pltpu.make_async_copy(d_ref.at[r], d_hbm.at[r], d_sems.at[r]))
    for copy in copies:
        copy.wait()


def dx_kernel(core_ref, mine_ref, other_ref, d_ref, w_ref, keep_ref, send_ref, norm_ref):
    core = core_ref[0]
    groups, blocks, cols = 8, 16, 32
    n, half = blocks * cols, cols // 2
    norm_ref[...] = jnp.zeros_like(norm_ref)

    def one_row(r, carry):
        src = pl.ds(r * blocks, blocks)
        mine = mine_ref[src, 0:cols, :].reshape(n, C)
        pair = jnp.where(core == 0, mine, other_ref[src, :, :].reshape(n, C))
        normed, _ = normalize(pair.astype(F32))
        dx = dot_tn(d_ref[r], w_ref[0:256, :])
        norm_ref[0:8, :] += jnp.sum((dx * normed).reshape(n // 8, 8, C), axis=0)
        norm_ref[8:16, :] += jnp.sum(dx.reshape(n // 8, 8, C), axis=0)
        dx = dx.astype(BF16).reshape(blocks, cols, C)
        keep_ref[src] = jnp.where(core == 0, dx[:, 0:half], dx[:, half:cols])
        send_ref[src] = jnp.where(core == 0, dx[:, half:cols], dx[:, 0:half])
        return carry

    lax.fori_loop(0, groups, one_row, 0, unroll=2)


def merge_kernel(keep_ref, came_ref, nt_ref, out_ref):
    devices, half = keep_ref.shape[0], keep_ref.shape[1]
    out_ref[:, 0:half, :] = nt_ref[...].reshape(devices, half, C)
    both = keep_ref[...].astype(F32) + came_ref[...].astype(F32)
    out_ref[:, half : 2 * half, :] = both.astype(BF16)


def sums_kernel(
    core_ref, held_ref, got_ref, norm_ref, gain_ref, shift_ref, wb_ref,
    z_ref, sums_hbm, z_scr, s_scr, sums_ref, sems,
):
    core = core_ref[0]
    rows, cols = got_ref.shape[0], 32
    last = pltpu.make_async_copy(held_ref.at[:, 16:32, :], sums_hbm.at[:, 16:32, :], sems.at[0])
    last.start()
    z_scr[...] = jnp.zeros_like(z_scr)
    for pair in range(2):

        def add(i, total, pair=pair):
            return total + got_ref[i, pair, 0:cols, :].astype(F32)

        total = lax.fori_loop(0, rows, add, jnp.zeros((cols, C), F32), unroll=8)
        for k in range(cols):
            for h in range(2):
                z_scr[2 * pair + h : 2 * pair + h + 1, k * rows : (k + 1) * rows] = total[
                    k : k + 1, h * 64 : (h + 1) * 64
                ]
    z = z_scr[...].astype(BF16)
    z_ref[...] = z
    nt = held_ref[:, 0:16, :].reshape(z.shape[1], C)
    dgn = dot_nn(z, nt)[0:4]
    total = jnp.sum(z_scr[0:4, :], axis=1, keepdims=True)

    def add_w(i, total):
        return total + got_ref[i, core, cols : cols + 8, :].astype(F32)

    s_scr[0:8, :] = lax.fori_loop(0, rows, add_w, jnp.zeros((8, C), F32), unroll=8)
    s_scr[8:12, :] = dgn * gain_ref[...] + total * shift_ref[...]
    wb = wb_ref[...].astype(F32)
    dgain = jnp.sum(norm_ref[0:8, :], axis=0, keepdims=True)
    dgain = dgain + jnp.sum(dgn * wb, axis=0, keepdims=True)
    dshift = jnp.sum(norm_ref[8:16, :], axis=0, keepdims=True)
    dshift = dshift + jnp.sum(total * wb, axis=0, keepdims=True)
    s_scr[12:13, :] = dgain
    s_scr[13:14, :] = dshift
    s_scr[14:15, :] = dgain - dgain.astype(BF16).astype(F32)
    s_scr[15:16, :] = dshift - dshift.astype(BF16).astype(F32)
    sums_ref[...] = jnp.broadcast_to(s_scr[...].astype(BF16)[None], sums_ref.shape)
    first = pltpu.make_async_copy(sums_ref, sums_hbm.at[:, 0:16, :], sems.at[1])
    first.start()
    last.wait()
    first.wait()


def ready_kernel(z_ref, pair_ref, gain_ref, wb_ref, ready_ref, dxb_scr, wb_scr):
    rows, cols = pair_ref.shape[0], pair_ref.shape[1]
    wb_scr[...] = jnp.zeros_like(wb_scr)
    wb_scr[0:4, :] = wb_ref[...].astype(F32)
    dxb_scr[...] = dot_tn(z_ref[...], wb_scr[...].astype(BF16))
    gain = gain_ref[...]

    def some(it, carry):
        i0 = it * 8
        part = pl.ds(i0, 8)
        normed, rstd = normalize(pair_ref[part].astype(F32))
        ready_ref[part, cols : 2 * cols, :] = normed.astype(BF16)
        ready_ref[part, 2 * cols : 3 * cols, :] = jnp.broadcast_to(rstd, normed.shape).astype(BF16)
        dxb = [dxb_scr[pl.ds(i0 + u, cols, stride=rows), :][None] for u in range(8)]
        dn = jnp.concatenate(dxb, axis=0) * gain
        base = rstd * (
            dn
            - jnp.mean(dn, axis=-1, keepdims=True)
            - normed * jnp.mean(dn * normed, axis=-1, keepdims=True)
        )
        ready_ref[part, 0:cols, :] = base.astype(BF16)
        return carry

    lax.fori_loop(0, rows // 8, some, 0)


def final_kernel(
    ready_ref, got_ref, gain_ref,
    dpair_hbm, dgain_ref, dshift_ref, dq_hbm, dk_hbm, dv_hbm, dg_hbm, db_ref, do_hbm,
    w_scr, dpair_ref, turn_scr, out_sems, w_sems,
):
    chips, cols, parts = got_ref.shape[0], dpair_ref.shape[1], out_sems.shape[0]
    size = chips // parts
    for core in range(2):
        for i in range(chips):
            w_scr[core, 5 * i : 5 * i + 8, :] = got_ref[i, core, 0:16, :].astype(F32)[0:8]
    sent = []
    for slot, out in enumerate((dq_hbm, dg_hbm, dk_hbm, dv_hbm)):
        sl = slice(slot * 64, (slot + 1) * 64)
        heads = jnp.concatenate([w_scr[0, sl, :], w_scr[1, sl, :]], axis=0)
        turn_scr[slot] = jnp.transpose(heads)
        sent.append(pltpu.make_async_copy(turn_scr.at[slot], out, w_sems.at[slot]))
    turn_scr[4, 0:64, :] = w_scr[0, 256:320, :]
    turn_scr[4, 64:128, :] = w_scr[1, 256:320, :]
    sent.append(pltpu.make_async_copy(turn_scr.at[4], do_hbm, w_sems.at[4]))
    for copy in sent:
        copy.start()
    zero = jnp.zeros((16, C), F32)

    def add(i, total):
        return total + (got_ref[i, 0, 0:16, :].astype(F32) + got_ref[i, 1, 0:16, :].astype(F32))

    total = lax.fori_loop(0, chips, add, zero, unroll=8)
    db_ref[...] = total[8:12]
    dgain_ref[...] = total[12:13] + total[14:15]
    dshift_ref[...] = total[13:14] + total[15:16]
    gain = gain_ref[...]
    for p in range(parts):
        part = pl.ds(p * size, size)
        normed = ready_ref[part, cols : 2 * cols, :].astype(F32).reshape(size * cols, C)
        dx = jnp.concatenate([got_ref[part, 0, 16:32, :], got_ref[part, 1, 16:32, :]], axis=1)
        dn = dx.astype(F32).reshape(size * cols, C) * gain
        out = dn - mean_lanes(dn) - normed * mean_lanes(dn * normed)
        rstd = ready_ref[part, 2 * cols : 3 * cols, :].astype(F32)
        out = out.reshape(size, cols, C) * rstd + ready_ref[part, 0:cols, :].astype(F32)
        dpair_ref[part] = out.astype(BF16)
        sent.append(pltpu.make_async_copy(dpair_ref.at[part], dpair_hbm.at[part], out_sems.at[p]))
        sent[-1].start()
    for copy in sent:
        copy.wait()


def on_device(
    pair, grad_out, norm_gain, norm_shift, w_query, w_key, w_value, w_gate, w_bias, w_out
):
    axes = ("row", "col")
    rows, cols = pair.shape[0], pair.shape[1]
    devices = 2 * rows
    sds = jax.ShapeDtypeStruct
    gain, shift = norm_gain.reshape(1, C), norm_shift.reshape(1, C)
    wb = w_bias.T
    core = (lax.axis_index("col") % 2).astype(jnp.int32).reshape(1)

    turned_scr = pltpu.VMEM((rows * cols, C), BF16)
    packed, nt = call(
        pack_kernel,
        (sds((rows, 2, 64, C), BF16), sds((rows * cols, C), BF16)),
        0,
        (
            pltpu.VMEM((rows * cols, C), F32),
            pltpu.VMEM((cols, C), F32),
            pltpu.VMEM((1, C), F32),
            pltpu.VMEM((1, C), F32),
            pltpu.VMEM((H, C), BF16),
            turned_scr,
            pltpu.SemaphoreType.DMA((6,)),
        ),
        hbm=5,
        flops=10**8,
        moved=4 * MIB,
    )(*(in_hbm(a) for a in (pair, grad_out, gain, shift, wb)))
    mine = lax.all_to_all(packed.reshape(devices, 64, C), axes, 0, 0, tiled=True)
    swap = [(i, i ^ 1) for i in range(16)]
    other = lax.ppermute(mine[:, 0:cols, :], "col", swap)
    bias, turned_w = call(
        prepare_kernel,
        (sds((2, 512, 512), F32), sds((320, C), BF16)),
        6,
        smem=1,
        flops=10**8,
        moved=4 * MIB,
    )(core, mine, w_query, w_key, w_value, w_gate, w_out)
    terms, spread = call(
        attend_kernel,
        (pltpu.HBM((devices, 40, C), BF16), pltpu.HBM((8, 256, 512), BF16)),
        6,
        (
            pltpu.VMEM((2, 512, 512), F32),
            pltpu.VMEM((328, C), F32),
            pltpu.VMEM((16, C, 512), BF16),
            pltpu.VMEM((devices, 40, C), BF16),
            pltpu.VMEM((8, 256, 512), BF16),
            pltpu.SemaphoreType.DMA((4,)),
            pltpu.SemaphoreType.DMA((8,)),
        ),
        smem=1,
        to_hbm=(0, 1),
        vmem=24,
        flops=10**10,
        moved=6 * MIB,
    )(core, mine, other, gain, shift, bias, turned_w)
    got = lax.all_to_all(terms, axes, 0, 0, tiled=True).reshape(rows, 2, 40, C)
    halves = sds((devices, cols // 2, C), BF16)
    keep, send, norms = call(
        dx_kernel,
        (halves, halves, sds((16, C), F32)),
        4,
        smem=1,
        flops=10**9,
        moved=6 * MIB,
    )(core, mine, other, spread, turned_w)
    came = lax.ppermute(send, "col", swap)
    held = call(
        merge_kernel, sds((devices, cols, C), BF16), 3, flops=10**7, moved=2 * MIB
    )(keep, came, nt)
    z, sums = call(
        sums_kernel,
        (sds((8, rows * cols), BF16), pltpu.HBM((devices, 32, C), BF16)),
        6,
        (
            pltpu.VMEM((8, rows * cols), F32),
            pltpu.VMEM((16, C), F32),
            pltpu.VMEM((devices, 16, C), BF16),
            pltpu.SemaphoreType.DMA((2,)),
        ),
        smem=1,
        to_hbm=(1,),
        flops=10**8,
        moved=4 * MIB,
    )(core, held, got, norms, gain, shift, wb)
    last = lax.all_to_all(sums, axes, 0, 0, tiled=True).reshape(rows, 2, 32, C)
    ready = call(
        ready_kernel,
        sds((rows, 3 * cols, C), BF16),
        4,
        (pltpu.VMEM((rows * cols, C), F32), pltpu.VMEM((8, C), F32)),
        flops=10**8,
        moved=8 * MIB,
    )(z, pair, gain, wb)
    square = pltpu.HBM((C, C), F32)
    d_pair, d_gain, d_shift, d_query, d_key, d_value, d_gate, d_bias, d_out = call(
        final_kernel,
        (
            pltpu.HBM(pair.shape, BF16),
            sds((1, C), F32),
            sds((1, C), F32),
            square,
            square,
            square,
            square,
            sds((H, C), F32),
            square,
        ),
        3,
        (
            pltpu.VMEM((2, 328, C), F32),
            pltpu.VMEM(pair.shape, BF16),
            pltpu.VMEM((5, C, C), F32),
            pltpu.SemaphoreType.DMA((8,)),
            pltpu.SemaphoreType.DMA((5,)),
        ),
        to_hbm=(0, 3, 4, 5, 6, 8),
        moved=8 * MIB,
    )(ready, last, gain)
    return (
        d_pair,
        d_gain.reshape(C),
        d_shift.reshape(C),
        d_query,
        d_key,
        d_value,
        d_gate,
        d_bias.T,
        d_out,
    )


def solution(mesh):
    return jax.shard_map(
        on_device,
        mesh=mesh,
        in_specs=(P("row", "col", None), P("row", "col", None)) + (P(),) * 8,
        out_specs=(P("row", "col", None),) + (P(),) * 8,
        check_vma=False,
    )
```
